256 devices in a mesh: seq: 256 (over y, x, z, core).
Axes of the slice: x: 4, y: 4, z: 8, core: 2. Of those that a mesh axis runs over, the one named last changes fastest.
Arguments:
- query_rows: bfloat16 [65536, 1024], P('seq'), may hold values from -16 to 16
- key_rows: bfloat16 [65536, 1024], P('seq'), may hold values from -16 to 16
- value_rows: bfloat16 [65536, 1024], P('seq'), may hold values from -6 to 6
Outputs:
- attended: bfloat16 [65536, 1024], P('seq')
The draws below stay inside these ranges and needn't reach their ends.
All inputs are finite; a program needn't handle non-finite values.
Results may differ from the reference program's by a relative error of at most 0.012.
The reference program's roundings to bfloat16 on the way (of `coarse_queries`, `coarse_keys`, `coarse_values` and `rounded`) count: a program that leaves them out, or rounds other values in their place, can miss the bound.
Values may be sent and summed in bfloat16 or wider, within the bound.
No kernel may reach another device: no remote copies, remote signals or barrier semaphores. Data moves between devices by JAX's collectives and lax.ppermute only.
A program may use at most 64 MiB of HBM per device.

```python
import math
import jax
import jax.numpy as jnp
from jax import lax

H = 8
DH = 128
B = 256
LEVELS = 5
TOKENS = 65536


def draw_query_rows(key, part):
    key = jax.random.fold_in(key, 5)
    rough_part = 1.5 * jax.random.truncated_normal(key, -4.0, 4.0, (TOKENS, H * DH), jnp.float32)
    return rough_part.astype(jnp.bfloat16)


def draw_key_rows(key, part):
    key = jax.random.fold_in(key, 7)
    rough_part = 1.5 * jax.random.truncated_normal(key, -4.0, 4.0, (TOKENS, H * DH), jnp.float32)
    return rough_part.astype(jnp.bfloat16)


def draw_value_rows(key, part):
    key = jax.random.fold_in(key, 9)
    rough_key, period_key, phase_key, amplitude_key = jax.random.split(key, 4)
    positions = jnp.arange(TOKENS, dtype=jnp.float32)
    periods = B * 2.0 ** jax.random.uniform(period_key, (H * DH,), jnp.float32, 0.0, LEVELS + 1.0)
    phases = jax.random.uniform(phase_key, (H * DH,), jnp.float32, 0.0, 2.0 * math.pi)
    amplitude = jax.random.uniform(amplitude_key, (H * DH,), jnp.float32, 0.5, 1.5)
    smooth_part = amplitude[None, :] * jnp.sin(2.0 * math.pi * positions[:, None] / periods[None, :] + phases[None, :])
    rough_part = jax.random.truncated_normal(rough_key, -4.0, 4.0, (TOKENS, H * DH), jnp.float32)
    return (rough_part + smooth_part).astype(jnp.bfloat16)


def setup_inputs(seed: int = 0) -> dict:
    arg_keys = jax.random.split(jax.random.key(seed), 4)
    query_rows = draw_query_rows(jax.random.fold_in(arg_keys[3], 71), 0)
    key_rows = draw_key_rows(jax.random.fold_in(arg_keys[3], 71), 0)
    value_rows = draw_value_rows(jax.random.fold_in(arg_keys[3], 71), 0)
    return dict(query_rows=query_rows, key_rows=key_rows, value_rows=value_rows)


MASKED_SCORE = -1e+30

def attend(queries, key_block, value_block, usable, multiple):
    row_count = queries.shape[0]
    key_count = key_block.shape[0]
    head_size = queries.shape[1] // H
    query_split = queries.astype(jnp.float32).reshape(row_count, H, head_size)
    key_split = key_block.astype(jnp.float32).reshape(key_count, H, head_size)
    value_split = value_block.astype(jnp.float32).reshape(key_count, H, head_size)
    scores = jnp.einsum('qhd,khd->hqk', query_split, key_split, precision=lax.Precision.HIGHEST) / math.sqrt(head_size)
    scores = jnp.where(usable[None, None, :], scores, MASKED_SCORE)
    maxima = lax.optimization_barrier(jnp.max(scores, axis=2))
    weights = jnp.exp(scores - maxima[:, :, None])
    denominator = multiple * lax.optimization_barrier(jnp.sum(weights, axis=2))
    rounded = lax.optimization_barrier(weights.astype(jnp.bfloat16)).astype(jnp.float32)
    numerator = jnp.einsum('hqk,khd->qhd', rounded, value_split, precision=lax.Precision.HIGHEST)
    return (maxima.T, numerator, denominator.T)

def level_terms(query_rows, key_rows, value_rows, level_index):
    factor = 2 ** level_index
    coarse_count = query_rows.shape[0] // factor
    features = query_rows.shape[1]
    coarse_queries = lax.optimization_barrier(jnp.mean(query_rows.reshape(coarse_count, factor, features), axis=1, dtype=jnp.float32)).astype(jnp.bfloat16)
    coarse_keys = lax.optimization_barrier(jnp.mean(key_rows.reshape(coarse_count, factor, features), axis=1, dtype=jnp.float32)).astype(jnp.bfloat16)
    coarse_values = lax.optimization_barrier(jnp.sum(value_rows.reshape(coarse_count, factor, features), axis=1, dtype=jnp.float32)).astype(jnp.bfloat16)
    block_count = coarse_count // B
    query_blocks = coarse_queries.reshape(block_count, B, features)
    key_blocks = jnp.pad(coarse_keys, ((B, B), (0, 0))).reshape(block_count + 2, B, features)
    value_blocks = jnp.pad(coarse_values, ((B, B), (0, 0))).reshape(block_count + 2, B, features)

    def one_block(block_index):
        has_left = jnp.full((B,), block_index >= 1)
        has_right = jnp.full((B,), block_index <= block_count - 2)
        if level_index == 0:
            keys_here = jnp.concatenate([key_blocks[block_index], key_blocks[block_index + 1], key_blocks[block_index + 2]], axis=0)
            values_here = jnp.concatenate([value_blocks[block_index], value_blocks[block_index + 1], value_blocks[block_index + 2]], axis=0)
            usable = jnp.concatenate([has_left, jnp.ones((B,), jnp.bool_), has_right])
        else:
            keys_here = jnp.concatenate([key_blocks[block_index], key_blocks[block_index + 2]], axis=0)
            values_here = jnp.concatenate([value_blocks[block_index], value_blocks[block_index + 2]], axis=0)
            usable = jnp.concatenate([has_left, has_right])
        return attend(query_blocks[block_index], keys_here, values_here, usable, float(factor))
    maxima, numerator, denominator = lax.map(one_block, jnp.arange(block_count, dtype=jnp.int32))
    return (maxima.reshape(coarse_count, H), numerator.reshape(coarse_count, H, features // H), denominator.reshape(coarse_count, H))

def reference(query_rows, key_rows, value_rows):
    maxima, numerator, denominator = level_terms(query_rows, key_rows, value_rows, 0)
    for level_index in range(1, LEVELS):
        factor = 2 ** level_index
        level_max, level_num, level_den = level_terms(query_rows, key_rows, value_rows, level_index)
        level_max = jnp.repeat(level_max, factor, axis=0)
        level_num = jnp.repeat(level_num, factor, axis=0)
        level_den = jnp.repeat(level_den, factor, axis=0)
        combined = jnp.maximum(maxima, level_max)
        rescale_old = jnp.exp(maxima - combined)
        rescale_new = jnp.exp(level_max - combined)
        numerator = numerator * rescale_old[:, :, None] + level_num * rescale_new[:, :, None]
        denominator = denominator * rescale_old + level_den * rescale_new
        maxima = combined
    attended = numerator / denominator[:, :, None]
    return attended.reshape(numerator.shape[0], -1).astype(jnp.bfloat16)
```

```python
import functools
import math

import jax
import jax.numpy as jnp
from jax import lax
from jax.experimental import pallas as pl
from jax.experimental.pallas import tpu as pltpu
from jax.sharding import PartitionSpec as P

HEADS = 4
DH = 128
COLS = HEADS * DH
B = 256
PACK = COLS + 128
ABSENT = -1e30
SCALE = math.log2(math.e) / math.sqrt(DH)
F32 = jnp.float32
BF16 = jnp.bfloat16

CHIPS = 128
RING = 8
ROWS4, ROWS3 = 32, 64
SEND = 3 * ROWS4 + 2 * ROWS3
BACK = ROWS4 + ROWS3


def shaped(*shape):
    return jax.ShapeDtypeStruct(shape, BF16)


def call(body, outs, scalars, arrays, flops=0, size=0):
    return pl.pallas_call(
        body,
        out_shape=outs,
        in_specs=[pl.BlockSpec(memory_space=pltpu.SMEM)]
        + [pl.BlockSpec(memory_space=pltpu.VMEM)] * len(arrays),
        out_specs=jax.tree.map(lambda _: pl.BlockSpec(memory_space=pltpu.VMEM), outs),
        compiler_params=pltpu.CompilerParams(vmem_limit_bytes=56 * 2**20),
        cost_estimate=pl.CostEstimate(flops=flops, bytes_accessed=size, transcendentals=0),
    )(scalars, *arrays)


def pool_matrix(rows, width, level, scale):
    row = lax.broadcasted_iota(jnp.int32, (rows, width), 0)
    col = lax.broadcasted_iota(jnp.int32, (rows, width), 1)
    return jnp.where((col >> level) == row, scale, 0.0).astype(BF16)


def spread_matrix(rows, width, level):
    row = lax.broadcasted_iota(jnp.int32, (rows, width), 0)
    col = lax.broadcasted_iota(jnp.int32, (rows, width), 1)
    return jnp.where((row >> level) == col, 1.0, 0.0).astype(BF16)


def pooled(x, level, mean):
    scale = 1.0 / 2**level if mean else 1.0
    matrix = pool_matrix(B >> level, B, level, scale)
    return jnp.dot(matrix, x, preferred_element_type=F32).astype(BF16)


def attend(q, parts, factor):
    scores = []
    for k, _, bias in parts:
        s = lax.dot_general(q, k, (((1,), (1,)), ((), ())), preferred_element_type=F32) * SCALE
        scores.append(s if bias is None else s + bias)
    m = functools.reduce(jnp.maximum, [jnp.max(s, axis=1, keepdims=True) for s in scores])
    total, out = None, None
    for s, (_, v, _) in zip(scores, parts):
        w = jnp.exp2(s - m)
        t = jnp.sum(w, axis=1, keepdims=True)
        o = jnp.dot(w.astype(BF16), v, preferred_element_type=F32)
        total = t if total is None else total + t
        out = o if out is None else out + o
    total = total * factor
    return (out / total).astype(BF16), m + jnp.log2(total)


def tile_of(values):
    rows = values[0].shape[0]
    lane = lax.broadcasted_iota(jnp.int32, (rows, 128), 1)
    full = jnp.zeros((rows, 128), F32)
    for h, value in enumerate(values):
        full = jnp.where((lane & 3) == h, value, full)
    high = full.astype(BF16)
    rest = full - high.astype(F32)
    middle = rest.astype(BF16)
    low = (rest - middle.astype(F32)).astype(BF16)
    zero = jnp.zeros((rows, 128), BF16)
    part = lane >> 2
    return jnp.where(part == 0, high, jnp.where(part == 1, middle, jnp.where(part == 2, low, zero)))


def attend_to(out_ref, row, q_of, parts_of, rows, factor):
    values = []
    for h in range(HEADS):
        cols = slice(h * DH, (h + 1) * DH)
        o, value = attend(q_of(cols), parts_of(cols), factor)
        out_ref[row : row + rows, cols] = o
        values.append(value)
    out_ref[row : row + rows, COLS:] = tile_of(values)


def pool_body(s, q, k, v, got, fine, rpay, lpay, q1, ppay, apay):
    core, half = s[0], s[1]
    levels = {}
    for n, ref in enumerate((q, k, v)):
        own = ref[...]
        other = got[n]
        for at in (0, 1):
            x = jnp.where(core == at, own, other)
            fine[n, at * B : (at + 1) * B] = x
            for level in (1, 2, 3, 4):
                levels[n, at, level] = pooled(x, level, n < 2)
            if n:
                to = rpay if at else lpay
                to[(n - 1) * B : n * B] = x
                to = lpay if at else rpay
                to[2 * B + (n - 1) * 128 : 2 * B + n * 128] = levels[n, at, 1]
    for at in (0, 1):
        q1[at * 128 : (at + 1) * 128] = levels[0, at, 1]
        for n in range(3):
            ppay[n * 128 + at * 64 : n * 128 + (at + 1) * 64] = levels[n, at, 2]
        for j in range(RING):
            cols = slice((j % HEADS) * DH, (j % HEADS + 1) * DH)
            for n in range(3):
                apay[j, n * ROWS4 + at * 16 : n * ROWS4 + (at + 1) * 16] = levels[n, at, 4][:, cols]
            first = jnp.where(
                half == j // HEADS, levels[0, at, 3][:, cols], levels[1, at, 3][:, cols]
            )
            base = 3 * ROWS4
            apay[j, base + at * 32 : base + (at + 1) * 32] = first
            base += ROWS3
            apay[j, base + at * 32 : base + (at + 1) * 32] = levels[2, at, 3][:, cols]


def near_body(s, fine, out):
    for at in (0, 1):
        rows = slice(at * B, (at + 1) * B)
        attend_to(
            out,
            at * B,
            lambda cols: fine[0, rows, cols],
            lambda cols: [(fine[1, :, cols], fine[2, :, cols], None)],
            B,
            1.0,
        )


def far_body(s, fine, q1, rin, lin, out0, out1):
    has_left, has_right = s[2], s[3]
    bias_left = jnp.where(has_left == 1, 0.0, ABSENT).astype(F32)
    bias_right = jnp.where(has_right == 1, 0.0, ABSENT).astype(F32)
    for at, ref, bias in ((0, rin, bias_left), (1, lin, bias_right)):
        attend_to(
            out0,
            at * B,
            lambda cols: fine[0, at * B : (at + 1) * B, cols],
            lambda cols: [(ref[:B, cols], ref[B : 2 * B, cols], bias)],
            B,
            1.0,
        )

    def coarse(cols):
        parts = []
        for ref, bias in ((rin, bias_left), (lin, bias_right)):
            keys = pooled(ref[:B, cols], 1, True)
            values = pooled(ref[B : 2 * B, cols], 1, False)
            parts.append((keys, values, bias))
            parts.append((ref[2 * B : 2 * B + 128, cols], ref[2 * B + 128 :, cols], bias))
        return parts

    attend_to(out1, 0, lambda cols: q1[:, cols], coarse, B, 2.0)


def pair_body(s, ppay, pin, bin_, out):
    bias = jnp.where(s[4] == 1, 0.0, ABSENT).astype(F32)
    for row, ref in ((0, ppay), (128, pin)):
        attend_to(
            out,
            row,
            lambda cols: ref[:128, cols],
            lambda cols: [
                (bin_[:128, cols], bin_[128:256, cols], bias),
                (bin_[256:384, cols], bin_[384:, cols], bias),
            ],
            128,
            4.0,
        )


def row_pay_body(s, ain, xpay):
    other = (1 - s[1]) * HEADS
    for j in range(RING):
        xpay[j * ROWS4 : (j + 1) * ROWS4] = ain[j, ROWS4 : 2 * ROWS4]
        xpay[B + j * ROWS4 : B + (j + 1) * ROWS4] = ain[j, 2 * ROWS4 : 3 * ROWS4]
    for j in range(HEADS):
        for n in (0, 1):
            base = 3 * ROWS4 + n * ROWS3
            to = (2 + n) * B + j * ROWS3
            xpay[to : to + ROWS3] = ain[other + j, base : base + ROWS3]


def row_body(s, ain, xin, back):
    half, head = s[1], s[5]
    bias = jnp.where(s[6] == 1, 0.0, ABSENT).astype(F32)
    mine, other = half * HEADS, (1 - half) * HEADS
    base = 3 * ROWS4
    rows3 = lambda at, low: jnp.concatenate(
        [ain[at + j, low : low + ROWS3] for j in range(HEADS)], axis=0
    )
    lane = lax.broadcasted_iota(jnp.int32, (B, 128), 1)

    def tile(value):
        high = value.astype(BF16)
        rest = value - high.astype(F32)
        middle = rest.astype(BF16)
        low = (rest - middle.astype(F32)).astype(BF16)
        zero = jnp.zeros((B, 128), F32)
        picked = jnp.where(
            lane == head,
            high.astype(F32),
            jnp.where(
                lane == head + 4,
                middle.astype(F32),
                jnp.where(lane == head + 8, low.astype(F32), zero),
            ),
        )
        return picked.astype(BF16)

    q4 = jnp.concatenate([ain[j, :ROWS4] for j in range(RING)], axis=0)
    o4, value4 = attend(q4, [(xin[:B], xin[B : 2 * B], bias)], 16.0)
    t4 = tile(value4)
    for j in range(RING):
        rows = slice(j * ROWS4, (j + 1) * ROWS4)
        back[j, :ROWS4, :DH] = o4[rows]
        back[j, :ROWS4, DH:] = t4[rows]
    o3, value3 = attend(
        rows3(mine, base),
        [
            (rows3(other, base), rows3(other, base + ROWS3), None),
            (xin[2 * B : 3 * B], xin[3 * B :], bias),
        ],
        8.0,
    )
    t3 = tile(value3)
    for j in range(RING):
        rows = slice((j % HEADS) * ROWS3, (j % HEADS + 1) * ROWS3)
        back[j, ROWS4:, :DH] = o3[rows]
        back[j, ROWS4:, DH:] = t3[rows]


def merge_body(s, near, far, one, two, two_back, row_back, mine, send):
    core, half = s[0], s[1]
    low = half * HEADS
    four = []
    for side in (0, 1):
        o = [row_back[side * HEADS + g, :ROWS4, :DH] for g in range(HEADS)]
        t = [row_back[side * HEADS + g, :ROWS4, DH:].astype(F32) for g in range(HEADS)]
        four.append(jnp.concatenate(o + [(t[0] + t[1] + t[2] + t[3]).astype(BF16)], axis=1))
    o = [row_back[low + g, ROWS4:, :DH] for g in range(HEADS)]
    t = [row_back[low + g, ROWS4:, DH:].astype(F32) for g in range(HEADS)]
    three = jnp.concatenate(o + [(t[0] + t[1] + t[2] + t[3]).astype(BF16)], axis=1)
    for at in (0, 1):
        terms = [near[at * B : (at + 1) * B].astype(F32), far[at * B : (at + 1) * B].astype(F32)]
        for level, values in (
            (1, one[at * 128 : (at + 1) * 128]),
            (2, two[at * 64 : (at + 1) * 64]),
            (2, two_back[at * 64 : (at + 1) * 64]),
            (3, three[at * 32 : (at + 1) * 32]),
            (4, four[0][at * 16 : (at + 1) * 16]),
            (4, four[1][at * 16 : (at + 1) * 16]),
        ):
            spread = spread_matrix(B, B >> level, level)
            terms.append(jnp.dot(spread, values, preferred_element_type=F32))
        weights = []
        for term in terms:
            t = term[:, COLS:]
            weights.append(t + pltpu.roll(t, 128 - 4, 1) + pltpu.roll(t, 128 - 8, 1))
        top = functools.reduce(jnp.maximum, weights)
        weights = [jnp.exp2(t - top) for t in weights]
        inverse = 1.0 / functools.reduce(jnp.add, weights)
        weights = [t * inverse for t in weights]
        for h in range(HEADS):
            cols = slice(h * DH, (h + 1) * DH)
            total = None
            for term, t in zip(terms, weights):
                part = term[:, cols] * t[:, h : h + 1]
                total = part if total is None else total + part
            total = total.astype(BF16)

            @pl.when(core == at)
            def _():
                mine[:, cols] = total

            @pl.when(core != at)
            def _():
                send[:, cols] = total


def pairs_of(target):
    pairs = []
    for chip in range(CHIPS):
        to = target(chip)
        if 0 <= to < CHIPS:
            pairs += [(2 * chip + core, 2 * to + core) for core in (0, 1)]
    return pairs


SWAP = [(i, i ^ 1) for i in range(2 * CHIPS)]
RIGHT = pairs_of(lambda chip: chip + 1)
LEFT = pairs_of(lambda chip: chip - 1)
PAIR = pairs_of(lambda chip: chip ^ 1)
BOUND = pairs_of(lambda chip: chip + 1 if chip % 2 else chip - 1)
ROW = pairs_of(lambda chip: chip + RING if chip % RING < RING // 2 else chip - RING)
LINES = [
    [2 * (row * RING + z) + core for z in range(RING)]
    for row in range(CHIPS // RING)
    for core in (0, 1)
]


def send_to(x, pairs):
    return lax.ppermute(x, "seq", pairs)


def line_swap(x):
    return lax.all_to_all(x, "seq", 0, 0, axis_index_groups=LINES)


def local(query_rows, key_rows, value_rows):
    position = lax.axis_index("seq")
    core = position % 2
    chip = position // 2
    z = chip % RING
    row = chip // RING
    half = z // HEADS
    odd = chip % 2
    has_left = chip >= 1
    has_right = chip <= CHIPS - 2
    has_pair = jnp.where(odd == 1, chip <= CHIPS - 3, chip >= 2)
    has_row = jnp.where(half == 0, row >= 1, row <= CHIPS // RING - 2)
    s = jnp.stack(
        [core, half, has_left, has_right, has_pair, z % HEADS, has_row, odd]
    ).astype(jnp.int32)

    arrays = (query_rows, key_rows, value_rows)
    outgoing = jnp.stack([lax.dynamic_slice(x, (0, (1 - core) * COLS), (B, COLS)) for x in arrays])
    own = [lax.dynamic_slice(x, (0, core * COLS), (B, COLS)) for x in arrays]
    got = send_to(outgoing, SWAP)
    fine, rpay, lpay, q1, ppay, apay = call(
        pool_body,
        (
            shaped(3, 2 * B, COLS),
            shaped(3 * B, COLS),
            shaped(3 * B, COLS),
            shaped(B, COLS),
            shaped(384, COLS),
            shaped(RING, SEND, DH),
        ),
        s,
        (*own, got),
    )
    pin = send_to(ppay, PAIR)
    ain = line_swap(apay)
    rin = send_to(rpay, RIGHT)
    lin = send_to(lpay, LEFT)
    near = call(near_body, shaped(2 * B, PACK), s, (fine,), 2**28, 2**21)
    bin_ = send_to(jnp.concatenate([ppay[128:], pin[128:]]), BOUND)
    xin = send_to(call(row_pay_body, shaped(4 * B, DH), s, (ain,)), ROW)
    two = call(pair_body, shaped(B, PACK), s, (ppay, pin, bin_), 2**26, 2**20)
    two_back = send_to(two[128:], PAIR)
    row_back = line_swap(call(row_body, shaped(RING, BACK, 2 * DH), s, (ain, xin), 2**26, 2**20))
    far, one = call(
        far_body, (shaped(2 * B, PACK), shaped(B, PACK)), s, (fine, q1, rin, lin), 2**28, 2**21
    )
    mine, send = call(
        merge_body,
        (shaped(B, COLS), shaped(B, COLS)),
        s,
        (near, far, one, two[:128], two_back, row_back),
        2**26,
        2**21,
    )
    theirs = send_to(send, SWAP)
    return jnp.where(
        core == 0,
        jnp.concatenate([mine, theirs], axis=1),
        jnp.concatenate([theirs, mine], axis=1),
    )


def solution(mesh):
    spec = P("seq", None)
    return jax.shard_map(
        local, mesh=mesh, in_specs=(spec, spec, spec), out_specs=spec, check_vma=False
    )
```

```python
import functools
import math

import jax
import jax.numpy as jnp
from jax import lax
from jax.experimental import pallas as pl
from jax.experimental.pallas import tpu as pltpu
from jax.sharding import PartitionSpec as P

HEADS = 4
DH = 128
COLS = HEADS * DH
B = 256
PACK = COLS + 128
ABSENT = -1e30
SCALE = math.log2(math.e) / math.sqrt(DH)
F32 = jnp.float32
BF16 = jnp.bfloat16

CHIPS = 128
RING = 8
ROWS4, ROWS3 = 32, 64
SEND = 3 * ROWS4 + 2 * ROWS3
BACK = ROWS4 + ROWS3 + 16
VMEM_LIMIT = 24 * 2**20


def shaped(*shape):
    return jax.ShapeDtypeStruct(shape, BF16)


def call(body, outs, scalars, arrays, halves=0, extra=()):
    def outer(s, *refs):
        whole, rest = refs[:halves], list(refs[halves:])
        if halves:
            *rest, held, sems = rest
            start = pl.multiple_of(s[0] * COLS, COLS)
            copies = [
                pltpu.make_async_copy(ref.at[:, pl.ds(start, COLS)], held.at[i], sems.at[i])
                for i, ref in enumerate(whole)
            ]
            for copy in copies:
                copy.start()
            for copy in copies:
                copy.wait()
            rest = [held.at[i] for i in range(halves)] + rest
        body(s, *rest)

    scratch = list(extra)
    if halves:
        scratch += [pltpu.VMEM((halves, B, COLS), BF16), pltpu.SemaphoreType.DMA((halves,))]
    return pl.pallas_call(
        outer,
        out_shape=outs,
        in_specs=[pl.BlockSpec(memory_space=pltpu.SMEM)]
        + [pl.BlockSpec(memory_space=pl.ANY)] * halves
        + [pl.BlockSpec(memory_space=pltpu.VMEM)] * (len(arrays) - halves),
        out_specs=[pl.BlockSpec(memory_space=pltpu.VMEM)] * len(outs),
        scratch_shapes=scratch,
        compiler_params=pltpu.CompilerParams(vmem_limit_bytes=VMEM_LIMIT),
        cost_estimate=pl.CostEstimate(flops=0, bytes_accessed=0, transcendentals=0),
    )(scalars, *arrays)


def pool_matrix(rows, width, level, scale):
    row = lax.broadcasted_iota(jnp.int32, (rows, width), 0)
    col = lax.broadcasted_iota(jnp.int32, (rows, width), 1)
    return jnp.where((col >> level) == row, scale, 0.0).astype(BF16)


def spread_matrix(rows, width, level):
    row = lax.broadcasted_iota(jnp.int32, (rows, width), 0)
    col = lax.broadcasted_iota(jnp.int32, (rows, width), 1)
    return jnp.where((row >> level) == col, 1.0, 0.0).astype(BF16)


def pooled(x, level, mean):
    rows = x.shape[0]
    scale = 1.0 / 2**level if mean else 1.0
    matrix = pool_matrix(rows >> level, rows, level, scale)
    return jnp.dot(matrix, x, preferred_element_type=F32).astype(BF16)


def attend(jobs, factor):
    results = []
    scores = []
    for q, parts in jobs:
        row = []
        for k, _, bias in parts:
            s = lax.dot_general(q, k, (((1,), (1,)), ((), ())), preferred_element_type=F32) * SCALE
            row.append(s if bias is None else s + bias)
        scores.append(row)
    tops = [
        functools.reduce(jnp.maximum, [jnp.max(s, axis=1, keepdims=True) for s in row])
        for row in scores
    ]
    weights = [[jnp.exp2(s - m) for s in row] for row, m in zip(scores, tops)]
    totals = [
        functools.reduce(jnp.add, [jnp.sum(w, axis=1, keepdims=True) for w in row]) * factor
        for row in weights
    ]
    for (_, parts), row, m, total in zip(jobs, weights, tops, totals):
        out = None
        for w, (_, v, _) in zip(row, parts):
            o = jnp.dot(w.astype(BF16), v, preferred_element_type=F32)
            out = o if out is None else out + o
        results.append(((out / total).astype(BF16), m + jnp.log2(total)))
    return results


def tile_of(values):
    rows = values[0].shape[0]
    lane = lax.broadcasted_iota(jnp.int32, (rows, 128), 1)
    full = jnp.zeros((rows, 128), F32)
    for h, value in enumerate(values):
        full = jnp.where((lane & 3) == h, value, full)
    high = full.astype(BF16)
    rest = full - high.astype(F32)
    middle = rest.astype(BF16)
    low = (rest - middle.astype(F32)).astype(BF16)
    zero = jnp.zeros((rows, 128), BF16)
    part = lane >> 2
    return jnp.where(part == 0, high, jnp.where(part == 1, middle, jnp.where(part == 2, low, zero)))


def merged(terms):
    top = functools.reduce(jnp.maximum, [t for _, t in terms])
    weights = [jnp.exp2(t - top) for _, t in terms]
    total = functools.reduce(jnp.add, weights)
    inverse = 1.0 / total
    weights = [t * inverse for t in weights]
    outs = []
    for h in range(HEADS):
        cols = slice(h * DH, (h + 1) * DH)
        parts = [o[:, cols] * t[:, h : h + 1] for (o, _), t in zip(terms, weights)]
        outs.append(functools.reduce(jnp.add, parts))
    return outs, top + jnp.log2(total)


def unpacked(values):
    values = values.astype(F32)
    t = values[:, COLS:]
    return values[:, :COLS], t + pltpu.roll(t, 128 - 4, 1) + pltpu.roll(t, 128 - 8, 1)


def packed_tile(full):
    lane = lax.broadcasted_iota(jnp.int32, full.shape, 1)
    full = jnp.where(lane < HEADS, full, 0.0)
    high = full.astype(BF16).astype(F32)
    middle = (full - high).astype(BF16).astype(F32)
    low = (full - high - middle).astype(BF16).astype(F32)
    return (high + pltpu.roll(middle, 4, 1) + pltpu.roll(low, 8, 1)).astype(BF16)


def spread(values, rows, level):
    matrix = spread_matrix(rows, rows >> level, level)
    return unpacked(jnp.dot(matrix, values, preferred_element_type=F32))


def attend_to(out_ref, row, q_of, parts_of, rows, factor, group=2):
    values = []
    for first in range(0, HEADS, group):
        spans = [slice(h * DH, (h + 1) * DH) for h in range(first, first + group)]
        for cols, (o, value) in zip(
            spans, attend([(q_of(cols), parts_of(cols)) for cols in spans], factor)
        ):
            out_ref[row : row + rows, cols] = o
            values.append(value)
    out_ref[row : row + rows, COLS:] = tile_of(values)


def edge_body(s, k0, v0, k1, v1, rpay, lpay):
    low_first = s[0] == 0
    for n, pair in enumerate(((k0, k1), (v0, v1))):
        low = jnp.where(low_first, pair[0][...], pair[1][...])
        high = jnp.where(low_first, pair[1][...], pair[0][...])
        rpay[n * B : (n + 1) * B] = high
        lpay[n * B : (n + 1) * B] = low
        rows = slice(2 * B + n * 128, 2 * B + (n + 1) * 128)
        rpay[rows] = pooled(low, 1, n == 0)
        lpay[rows] = pooled(high, 1, n == 0)


def pool_body(s, q0, k0, v0, q1, k1, v1, q_one, q_two, apay):
    half = s[1]
    for at, refs in enumerate(((q0, k0, v0), (q1, k1, v1))):
        q = refs[0][...]
        q_one[at * 128 : (at + 1) * 128] = pooled(q, 1, True)
        q_two[at * 64 : (at + 1) * 64] = pooled(q, 2, True)
        three = [pooled(ref[...], 3, n < 2) for n, ref in enumerate(refs)]
        four = [pooled(ref[...], 4, n < 2) for n, ref in enumerate(refs)]
        for j in range(RING):
            cols = slice((j % HEADS) * DH, (j % HEADS + 1) * DH)
            for n in range(3):
                apay[j, n * ROWS4 + at * 16 : n * ROWS4 + (at + 1) * 16] = four[n][:, cols]
            first = jnp.where(half == j // HEADS, three[0][:, cols], three[1][:, cols])
            base = 3 * ROWS4
            apay[j, base + at * 32 : base + (at + 1) * 32] = first
            base += ROWS3
            apay[j, base + at * 32 : base + (at + 1) * 32] = three[2][:, cols]


def near_body(s, q0, k0, v0, q1, k1, v1, out):
    for at, q in enumerate((q0, q1)):
        attend_to(
            out,
            at * B,
            lambda cols: q[:, cols],
            lambda cols: [(k0[:, cols], v0[:, cols], None), (k1[:, cols], v1[:, cols], None)],
            B,
            1.0,
        )


def derive_body(s, rin, lin, bpay, kept):
    odd = s[7] == 1
    for n in (0, 1):
        sides = []
        for ref in (rin, lin):
            near = pooled(ref[n * B : (n + 1) * B], 2, n == 0)
            far = pooled(ref[2 * B + n * 128 : 2 * B + (n + 1) * 128], 1, n == 0)
            sides.append((near, far))
        for i in (0, 1):
            rows = slice(n * 128 + i * 64, n * 128 + (i + 1) * 64)
            bpay[rows] = jnp.where(odd, sides[0][i], sides[1][i])
            kept[rows] = jnp.where(odd, sides[1][i], sides[0][i])


def far_body(s, q0, q1, q_one, near, rin, lin, out, tile, out0, out1):
    first = s[0] == 0
    bias_left = jnp.where(s[2] == 1, 0.0, ABSENT).astype(F32)
    bias_right = jnp.where(s[3] == 1, 0.0, ABSENT).astype(F32)
    for at, q in enumerate((q0, q1)):
        left = first if at == 0 else jnp.logical_not(first)
        bias = jnp.where(left, bias_left, bias_right)
        attend_to(
            out0,
            at * B,
            lambda cols: q[:, cols],
            lambda cols: [
                (
                    jnp.where(left, rin[:B, cols], lin[:B, cols]),
                    jnp.where(left, rin[B : 2 * B, cols], lin[B : 2 * B, cols]),
                    bias,
                )
            ],
            B,
            1.0,
        )

    def coarse(cols):
        parts = []
        for ref, bias in ((rin, bias_left), (lin, bias_right)):
            keys = pooled(ref[:B, cols], 1, True)
            values = pooled(ref[B : 2 * B, cols], 1, False)
            keys = jnp.concatenate([keys, ref[2 * B : 2 * B + 128, cols]], axis=0)
            values = jnp.concatenate([values, ref[2 * B + 128 :, cols]], axis=0)
            parts.append((keys, values, bias))
        return parts

    attend_to(out1, 0, lambda cols: q_one[:, cols], coarse, B, 2.0)
    for at in (0, 1):
        rows = slice(at * B, (at + 1) * B)
        one = spread(out1[at * 128 : (at + 1) * 128], B, 1)
        outs, weights = merged([unpacked(near[rows]), unpacked(out0[rows]), one])
        for h in range(HEADS):
            out[rows, h * DH : (h + 1) * DH] = outs[h]
        tile[rows] = weights


def pair_body(s, q_two, kept, pin, bin_, mine, theirs):
    bias = jnp.where(s[4] == 1, 0.0, ABSENT).astype(F32)
    for out, ref in ((mine, q_two), (theirs, pin)):
        attend_to(
            out,
            0,
            lambda cols: ref[:, cols],
            lambda cols: [
                (
                    jnp.concatenate([kept[:128, cols], bin_[:128, cols]], axis=0),
                    jnp.concatenate([kept[128:, cols], bin_[128:, cols]], axis=0),
                    bias,
                ),
            ],
            128,
            4.0,
            4,
        )


def row_pay_body(s, ain, xpay):
    other = (1 - s[1]) * HEADS
    for j in range(RING):
        xpay[j * ROWS4 : (j + 1) * ROWS4] = ain[j, ROWS4 : 2 * ROWS4]
        xpay[B + j * ROWS4 : B + (j + 1) * ROWS4] = ain[j, 2 * ROWS4 : 3 * ROWS4]
    for j in range(HEADS):
        for n in (0, 1):
            base = 3 * ROWS4 + n * ROWS3
            to = (2 + n) * B + j * ROWS3
            xpay[to : to + ROWS3] = ain[other + j, base : base + ROWS3]


def row_body(s, ain, xin, back):
    half, head = s[1], s[5]
    bias = jnp.where(s[6] == 1, 0.0, ABSENT).astype(F32)
    mine, other = half * HEADS, (1 - half) * HEADS
    base = 3 * ROWS4
    rows3 = lambda at, low: jnp.concatenate(
        [ain[at + j, low : low + ROWS3] for j in range(HEADS)], axis=0
    )
    q4 = jnp.concatenate([ain[j, :ROWS4] for j in range(RING)], axis=0)
    ((o4, value4),) = attend([(q4, [(xin[:B], xin[B : 2 * B], bias)])], 16.0)
    parts = [
        (rows3(other, base), rows3(other, base + ROWS3), None),
        (xin[2 * B : 3 * B], xin[3 * B :], bias),
    ]
    ((o3, value3),) = attend([(rows3(mine, base), parts)], 8.0)
    row = lax.broadcasted_iota(jnp.int32, (ROWS4 + ROWS3, 128), 0)
    col = lax.broadcasted_iota(jnp.int32, (ROWS4 + ROWS3, 128), 1)
    term = lax.broadcasted_iota(jnp.int32, (16, 128), 0)
    for j in range(RING):
        rows4 = slice(j * ROWS4, (j + 1) * ROWS4)
        rows3 = slice((j % HEADS) * ROWS3, (j % HEADS + 1) * ROWS3)
        back[j, :ROWS4] = o4[rows4]
        back[j, ROWS4 : ROWS4 + ROWS3] = o3[rows3]
        values = jnp.concatenate([value4[rows4], value3[rows3]], axis=0)
        line = jnp.sum(jnp.where(row == col, values, 0.0), axis=0, keepdims=True)
        high = line.astype(BF16).astype(F32)
        middle = (line - high).astype(BF16).astype(F32)
        low = line - high - middle
        three = jnp.where(
            term == 0, high, jnp.where(term == 1, middle, jnp.where(term == 2, low, 0.0))
        )
        back[j, ROWS4 + ROWS3 :] = three.astype(BF16)


def merge_body(s, fine, tile, two, two_back, row_back, mine, send):
    low = s[1] * HEADS
    row = lax.broadcasted_iota(jnp.int32, (ROWS4 + ROWS3, 128), 0)
    lane = lax.broadcasted_iota(jnp.int32, (ROWS4 + ROWS3, 128), 1)

    def joined(first, rows):
        tile = jnp.zeros((ROWS4 + ROWS3, 128), F32)
        for g in range(HEADS):
            three = row_back[first + g, ROWS4 + ROWS3 :].astype(F32)
            line = jnp.sum(three, axis=0, keepdims=True)
            column = jnp.sum(jnp.where(row == lane, line, 0.0), axis=1, keepdims=True)
            tile = jnp.where(lane == g, column, tile)
        o = [row_back[first + g, rows] for g in range(HEADS)]
        return jnp.concatenate(o + [packed_tile(tile[rows])], axis=1)

    four = [joined(side * HEADS, slice(0, ROWS4)) for side in (0, 1)]
    three = joined(low, slice(ROWS4, ROWS4 + ROWS3))
    terms = [
        unpacked(two[...]),
        unpacked(two_back[...]),
        spread(three, 128, 1),
        spread(four[0], 128, 2),
        spread(four[1], 128, 2),
    ]
    outs, weights = merged(terms)
    coarse = jnp.concatenate([o.astype(BF16) for o in outs] + [packed_tile(weights)], axis=1)
    for at, out in enumerate((mine, send)):
        rows = slice(at * B, (at + 1) * B)
        outs, _ = merged(
            [(fine[rows], tile[rows]), spread(coarse[at * 64 : (at + 1) * 64], B, 2)]
        )
        for h in range(HEADS):
            out[:, h * DH : (h + 1) * DH] = outs[h].astype(BF16)


def join_body(s, mine, theirs, out, sems):
    low = pl.multiple_of(s[0] * COLS, COLS)
    high = pl.multiple_of((1 - s[0]) * COLS, COLS)
    copies = [
        pltpu.make_async_copy(mine, out.at[:, pl.ds(low, COLS)], sems.at[0]),
        pltpu.make_async_copy(theirs, out.at[:, pl.ds(high, COLS)], sems.at[1]),
    ]
    for copy in copies:
        copy.start()
    for copy in copies:
        copy.wait()


def join(s, mine, theirs):
    return pl.pallas_call(
        join_body,
        out_shape=shaped(B, 2 * COLS),
        in_specs=[pl.BlockSpec(memory_space=pltpu.SMEM)]
        + [pl.BlockSpec(memory_space=pltpu.VMEM)] * 2,
        out_specs=pl.BlockSpec(memory_space=pl.ANY),
        scratch_shapes=[pltpu.SemaphoreType.DMA((2,))],
        compiler_params=pltpu.CompilerParams(vmem_limit_bytes=VMEM_LIMIT),
    )(s, mine, theirs)


def pairs_of(target):
    pairs = []
    for chip in range(CHIPS):
        to = target(chip)
        if 0 <= to < CHIPS:
            pairs += [(2 * chip + core, 2 * to + core) for core in (0, 1)]
    return pairs


SWAP = [(i, i ^ 1) for i in range(2 * CHIPS)]
RIGHT = pairs_of(lambda chip: chip + 1)
LEFT = pairs_of(lambda chip: chip - 1)
PAIR = pairs_of(lambda chip: chip ^ 1)
BOUND = pairs_of(lambda chip: chip + 1 if chip % 2 else chip - 1)
ROW = pairs_of(lambda chip: chip + RING if chip % RING < RING // 2 else chip - RING)
LINES = [
    [2 * (row * RING + z) + core for z in range(RING)]
    for row in range(CHIPS // RING)
    for core in (0, 1)
]


def send_to(x, pairs):
    return lax.ppermute(x, "seq", pairs)


def after(x, y):
    return lax.optimization_barrier((x, y))


def line_swap(x):
    return lax.all_to_all(x, "seq", 0, 0, axis_index_groups=LINES)


def local(query_rows, key_rows, value_rows):
    position = lax.axis_index("seq")
    core = position % 2
    chip = position // 2
    z = chip % RING
    row = chip // RING
    half = z // HEADS
    odd = chip % 2
    has_left = chip >= 1
    has_right = chip <= CHIPS - 2
    has_pair = jnp.where(odd == 1, chip <= CHIPS - 3, chip >= 2)
    has_row = jnp.where(half == 0, row >= 1, row <= CHIPS // RING - 2)
    s = jnp.stack(
        [core, half, has_left, has_right, has_pair, z % HEADS, has_row, odd]
    ).astype(jnp.int32)

    own = (query_rows, key_rows, value_rows)
    got = [None, send_to(key_rows, SWAP), send_to(value_rows, SWAP)]
    got[0] = send_to(query_rows, SWAP)
    fine = (*own, *got)
    rpay, lpay = call(
        edge_body, (shaped(3 * B, COLS), shaped(3 * B, COLS)), s, (*own[1:], *got[1:]), halves=4
    )
    rin = send_to(rpay, RIGHT)
    lin = send_to(lpay, LEFT)
    s, rpay = after(s, rpay)
    outs = (shaped(B, COLS), shaped(128, COLS), shaped(RING, SEND, DH))
    q_one, q_two, apay = call(pool_body, outs, s, fine, halves=6)
    ain = line_swap(apay)
    pin = send_to(q_two, PAIR)
    (near,) = call(near_body, (shaped(2 * B, PACK),), s, fine, halves=6)
    s, near = after(s, near)
    (xpay,) = call(row_pay_body, (shaped(4 * B, DH),), s, (ain,))
    xin = send_to(xpay, ROW)
    s, _ = after(s, xpay)
    bpay, kept = call(derive_body, (shaped(B, COLS), shaped(B, COLS)), s, (rin, lin))
    bin_ = send_to(bpay, BOUND)
    s, _ = after(s, bpay)
    far, far_tile = call(
        far_body,
        (jax.ShapeDtypeStruct((2 * B, COLS), F32), jax.ShapeDtypeStruct((2 * B, 128), F32)),
        s,
        (query_rows, got[0], q_one, near, rin, lin),
        halves=2,
        extra=[pltpu.VMEM((2 * B, PACK), BF16), pltpu.VMEM((B, PACK), BF16)],
    )
    s, far = after(s, far)
    two, theirs = call(
        pair_body, (shaped(128, PACK), shaped(128, PACK)), s, (q_two, kept, pin, bin_)
    )
    two_back = send_to(theirs, PAIR)
    s, two = after(s, two)
    (back,) = call(row_body, (shaped(RING, BACK, DH),), s, (ain, xin))
    row_back = line_swap(back)
    mine, send = call(
        merge_body,
        (shaped(B, COLS), shaped(B, COLS)),
        s,
        (far, far_tile, two, two_back, row_back),
    )
    return join(s, mine, send_to(send, SWAP))


def solution(mesh):
    spec = P("seq", None)
    return jax.shard_map(
        local, mesh=mesh, in_specs=(spec, spec, spec), out_specs=spec, check_vma=False
    )
```

```python
import functools
import math

import jax
import jax.numpy as jnp
from jax import lax
from jax.experimental import pallas as pl
from jax.experimental.pallas import tpu as pltpu
from jax.sharding import PartitionSpec as P

HEADS = 4
DH = 128
COLS = HEADS * DH
B = 256
PACK = COLS + 128
ABSENT = -1e30
SCALE = math.log2(math.e) / math.sqrt(DH)
F32 = jnp.float32
BF16 = jnp.bfloat16

CHIPS = 128
RING = 8
ROWS4, ROWS3 = 32, 64
SEND = 3 * ROWS4 + 2 * ROWS3
BACK = ROWS4 + ROWS3 + 16
VMEM_LIMIT = 10 * 2**20


def shaped(*shape):
    return jax.ShapeDtypeStruct(shape, BF16)


def call(body, outs, scalars, arrays, wide=(), extra=(), slow=False):
    def outer(s, *refs):
        start = pl.multiple_of(s[0] * COLS, COLS)
        refs = [
            ref.at[:, pl.ds(start, COLS)] if i in wide else ref for i, ref in enumerate(refs)
        ]
        body(s, *refs)

    return pl.pallas_call(
        outer,
        out_shape=[pltpu.HBM(o.shape, o.dtype) for o in outs] if slow else outs,
        in_specs=[pl.BlockSpec(memory_space=pltpu.SMEM)]
        + [pl.BlockSpec(memory_space=pltpu.VMEM)] * len(arrays),
        out_specs=[pl.BlockSpec(memory_space=pltpu.HBM if slow else pltpu.VMEM)] * len(outs),
        scratch_shapes=list(extra),
        compiler_params=pltpu.CompilerParams(vmem_limit_bytes=VMEM_LIMIT),
        cost_estimate=pl.CostEstimate(flops=0, bytes_accessed=0, transcendentals=0),
    )(scalars, *arrays)


def half_body(s, q, k, v, out, sems):
    start = pl.multiple_of(s[0] * COLS, COLS)
    copies = [
        pltpu.make_async_copy(ref.at[:, pl.ds(start, COLS)], out.at[i], sems.at[i])
        for i, ref in enumerate((q, k, v))
    ]
    for copy in copies:
        copy.start()
    for copy in copies:
        copy.wait()


def half_columns(s, arrays):
    return pl.pallas_call(
        half_body,
        out_shape=shaped(3, B, COLS),
        in_specs=[pl.BlockSpec(memory_space=pltpu.SMEM)]
        + [pl.BlockSpec(memory_space=pltpu.HBM)] * 3,
        out_specs=pl.BlockSpec(memory_space=pltpu.VMEM),
        scratch_shapes=[pltpu.SemaphoreType.DMA((3,))],
        compiler_params=pltpu.CompilerParams(vmem_limit_bytes=VMEM_LIMIT),
        cost_estimate=pl.CostEstimate(flops=0, bytes_accessed=0, transcendentals=0),
    )(s, *(pltpu.with_memory_space_constraint(x, pltpu.HBM) for x in arrays))


def pool_matrix(rows, width, level, scale):
    row = lax.broadcasted_iota(jnp.int32, (rows, width), 0)
    col = lax.broadcasted_iota(jnp.int32, (rows, width), 1)
    return jnp.where((col >> level) == row, scale, 0.0).astype(BF16)


def spread_matrix(rows, width, level):
    row = lax.broadcasted_iota(jnp.int32, (rows, width), 0)
    col = lax.broadcasted_iota(jnp.int32, (rows, width), 1)
    return jnp.where((row >> level) == col, 1.0, 0.0).astype(BF16)


def pooled(x, level, mean):
    rows = x.shape[0]
    scale = 1.0 / 2**level if mean else 1.0
    matrix = pool_matrix(rows >> level, rows, level, scale)
    return jnp.dot(matrix, x, preferred_element_type=F32).astype(BF16)


def attend(jobs, factor):
    results = []
    scores = []
    for q, parts in jobs:
        row = []
        for k, _, bias in parts:
            s = lax.dot_general(q, k, (((1,), (1,)), ((), ())), preferred_element_type=F32) * SCALE
            row.append(s if bias is None else s + bias)
        scores.append(row)
    tops = [
        functools.reduce(jnp.maximum, [jnp.max(s, axis=1, keepdims=True) for s in row])
        for row in scores
    ]
    weights = [[jnp.exp2(s - m) for s in row] for row, m in zip(scores, tops)]
    totals = [
        functools.reduce(jnp.add, [jnp.sum(w, axis=1, keepdims=True) for w in row]) * factor
        for row in weights
    ]
    for (_, parts), row, m, total in zip(jobs, weights, tops, totals):
        out = None
        for w, (_, v, _) in zip(row, parts):
            o = jnp.dot(w.astype(BF16), v, preferred_element_type=F32)
            out = o if out is None else out + o
        results.append(((out / total).astype(BF16), m + jnp.log2(total)))
    return results


def tile_of(values):
    rows = values[0].shape[0]
    lane = lax.broadcasted_iota(jnp.int32, (rows, 128), 1)
    full = jnp.zeros((rows, 128), F32)
    for h, value in enumerate(values):
        full = jnp.where((lane & 3) == h, value, full)
    high = full.astype(BF16)
    rest = full - high.astype(F32)
    middle = rest.astype(BF16)
    low = (rest - middle.astype(F32)).astype(BF16)
    zero = jnp.zeros((rows, 128), BF16)
    part = lane >> 2
    return jnp.where(part == 0, high, jnp.where(part == 1, middle, jnp.where(part == 2, low, zero)))


def merged(terms):
    top = functools.reduce(jnp.maximum, [t for _, t in terms])
    weights = [jnp.exp2(t - top) for _, t in terms]
    total = functools.reduce(jnp.add, weights)
    inverse = 1.0 / total
    weights = [t * inverse for t in weights]
    outs = []
    for h in range(HEADS):
        cols = slice(h * DH, (h + 1) * DH)
        parts = [o[:, cols] * t[:, h : h + 1] for (o, _), t in zip(terms, weights)]
        outs.append(functools.reduce(jnp.add, parts))
    return outs, top + jnp.log2(total)


def unpacked(values):
    values = values.astype(F32)
    t = values[:, COLS:]
    return values[:, :COLS], t + pltpu.roll(t, 128 - 4, 1) + pltpu.roll(t, 128 - 8, 1)


def packed_tile(full):
    lane = lax.broadcasted_iota(jnp.int32, full.shape, 1)
    full = jnp.where(lane < HEADS, full, 0.0)
    high = full.astype(BF16).astype(F32)
    middle = (full - high).astype(BF16).astype(F32)
    low = (full - high - middle).astype(BF16).astype(F32)
    return (high + pltpu.roll(middle, 4, 1) + pltpu.roll(low, 8, 1)).astype(BF16)


def spread(values, rows, level):
    matrix = spread_matrix(rows, rows >> level, level)
    return unpacked(jnp.dot(matrix, values, preferred_element_type=F32))


def attend_to(out_ref, row, q_of, parts_of, rows, factor, group=2):
    values = []
    for first in range(0, HEADS, group):
        spans = [slice(h * DH, (h + 1) * DH) for h in range(first, first + group)]
        for cols, (o, value) in zip(
            spans, attend([(q_of(cols), parts_of(cols)) for cols in spans], factor)
        ):
            out_ref[row : row + rows, cols] = o
            values.append(value)
    out_ref[row : row + rows, COLS:] = tile_of(values)


def edge_body(s, own, k1, v1, rout, lout, rpay, lpay, sems):
    copies = []
    for i, (pay, out) in enumerate(((rpay, rout), (lpay, lout))):
        first = s[0] == 1 - i
        for n, ref in enumerate((k1, v1)):
            mine, other = own[1 + n], ref[...]
            pay[n * B : (n + 1) * B] = jnp.where(first, mine, other)
            pay[2 * B + n * 128 : 2 * B + (n + 1) * 128] = pooled(
                jnp.where(first, other, mine), 1, n == 0
            )
        copies.append(pltpu.make_async_copy(pay, out, sems.at[i]))
        copies[-1].start()
    for copy in copies:
        copy.wait()


def pair_pay_body(s, own, q1, q_two):
    q_two[:64] = pooled(own[0], 2, True)
    q_two[64:] = pooled(q1[...], 2, True)


def pool_body(s, own, q1, k1, v1, apay):
    half = s[1]
    for at in (0, 1):
        whole = (own[0], own[1], own[2]) if at == 0 else (q1[...], k1[...], v1[...])
        three = [pooled(x, 3, n < 2) for n, x in enumerate(whole)]
        four = [pooled(x, 4, n < 2) for n, x in enumerate(whole)]
        for j in range(RING):
            cols = slice((j % HEADS) * DH, (j % HEADS + 1) * DH)
            for n in range(3):
                apay[j, n * ROWS4 + at * 16 : n * ROWS4 + (at + 1) * 16] = four[n][:, cols]
            first = jnp.where(half == j // HEADS, three[1][:, cols], three[0][:, cols])
            base = 3 * ROWS4
            apay[j, base + at * 32 : base + (at + 1) * 32] = first
            base += ROWS3
            apay[j, base + at * 32 : base + (at + 1) * 32] = three[2][:, cols]


def near_body(s, own, q1, k1, v1, out):
    k0, v0 = own.at[1], own.at[2]
    for at, q in enumerate((own.at[0], q1)):
        attend_to(
            out,
            at * B,
            lambda cols: q[:, cols],
            lambda cols: [(k0[:, cols], v0[:, cols], None), (k1[:, cols], v1[:, cols], None)],
            B,
            1.0,
        )


def level_two(ref, n):
    near = pooled(ref[n * B : (n + 1) * B], 2, n == 0)
    far = pooled(ref[2 * B + n * 128 : 2 * B + (n + 1) * 128], 1, n == 0)
    return jnp.concatenate([near, far], axis=0)


def derive_body(s, rin, lin, bpay):
    odd = s[7] == 1
    for n in (0, 1):
        bpay[n * 128 : (n + 1) * 128] = jnp.where(odd, level_two(rin, n), level_two(lin, n))


def sides(s):
    left = jnp.where(s[2] == 1, 0.0, ABSENT).astype(F32)
    right = jnp.where(s[3] == 1, 0.0, ABSENT).astype(F32)
    return left, right


def far_body(s, own, q1, rin, lin, out):
    first = s[0] == 0
    bias_left, bias_right = sides(s)
    for at, q in enumerate((own.at[0], q1)):
        left = first if at == 0 else jnp.logical_not(first)
        bias = jnp.where(left, bias_left, bias_right)
        attend_to(
            out,
            at * B,
            lambda cols: q[:, cols],
            lambda cols: [
                (
                    jnp.where(left, rin[:B, cols], lin[:B, cols]),
                    jnp.where(left, rin[B : 2 * B, cols], lin[B : 2 * B, cols]),
                    bias,
                )
            ],
            B,
            1.0,
        )


def one_body(s, own, q1, near, far, rin, lin, out, one):
    def coarse(cols):
        parts = []
        for ref, bias in zip((rin, lin), sides(s)):
            keys = pooled(ref[:B, cols], 1, True)
            values = pooled(ref[B : 2 * B, cols], 1, False)
            keys = jnp.concatenate([keys, ref[2 * B : 2 * B + 128, cols]], axis=0)
            values = jnp.concatenate([values, ref[2 * B + 128 :, cols]], axis=0)
            parts.append((keys, values, bias))
        return parts

    q_one = jnp.concatenate([pooled(own[0], 1, True), pooled(q1[...], 1, True)], axis=0)
    attend_to(one, 0, lambda cols: q_one[:, cols], coarse, B, 2.0)
    for at in (0, 1):
        rows = slice(at * B, (at + 1) * B)
        level_one = spread(one[at * 128 : (at + 1) * 128], B, 1)
        outs, weights = merged([unpacked(near[rows]), unpacked(far[rows]), level_one])
        for h in range(HEADS):
            out[rows, h * DH : (h + 1) * DH] = outs[h]
        out[rows, COLS:] = weights


def pair_body(s, q_two, rin, lin, pin, bin_, mine, theirs):
    bias = jnp.where(s[4] == 1, 0.0, ABSENT).astype(F32)
    odd = s[7] == 1
    kept = [
        jnp.concatenate(
            [
                jnp.where(odd, level_two(lin, n), level_two(rin, n)),
                bin_[n * 128 : (n + 1) * 128],
            ],
            axis=0,
        )
        for n in (0, 1)
    ]
    for out, ref in ((mine, q_two), (theirs, pin)):
        attend_to(
            out,
            0,
            lambda cols: ref[:, cols],
            lambda cols: [(kept[0][:, cols], kept[1][:, cols], bias)],
            128,
            4.0,
            4,
        )


def row_pay_body(s, ain, xpay):
    same = s[1] * HEADS
    for j in range(RING):
        xpay[j * ROWS4 : (j + 1) * ROWS4] = ain[j, ROWS4 : 2 * ROWS4]
        xpay[B + j * ROWS4 : B + (j + 1) * ROWS4] = ain[j, 2 * ROWS4 : 3 * ROWS4]
    for j in range(HEADS):
        for n in (0, 1):
            base = 3 * ROWS4 + n * ROWS3
            to = (2 + n) * B + j * ROWS3
            xpay[to : to + ROWS3] = ain[same + j, base : base + ROWS3]


def row_body(s, ain, xin, back):
    half, head = s[1], s[5]
    bias = jnp.where(s[6] == 1, 0.0, ABSENT).astype(F32)
    mine, other = half * HEADS, (1 - half) * HEADS
    base = 3 * ROWS4
    rows3 = lambda at, low: jnp.concatenate(
        [ain[at + j, low : low + ROWS3] for j in range(HEADS)], axis=0
    )
    q4 = jnp.concatenate([ain[j, :ROWS4] for j in range(RING)], axis=0)
    ((o4, value4),) = attend([(q4, [(xin[:B], xin[B : 2 * B], bias)])], 16.0)
    parts = [
        (rows3(mine, base), rows3(mine, base + ROWS3), None),
        (xin[2 * B : 3 * B], xin[3 * B :], bias),
    ]
    ((o3, value3),) = attend([(rows3(other, base), parts)], 8.0)
    row = lax.broadcasted_iota(jnp.int32, (ROWS4 + ROWS3, 128), 0)
    col = lax.broadcasted_iota(jnp.int32, (ROWS4 + ROWS3, 128), 1)
    term = lax.broadcasted_iota(jnp.int32, (16, 128), 0)
    for j in range(RING):
        rows4 = slice(j * ROWS4, (j + 1) * ROWS4)
        rows3 = slice((j % HEADS) * ROWS3, (j % HEADS + 1) * ROWS3)
        back[j, :ROWS4] = o4[rows4]
        back[j, ROWS4 : ROWS4 + ROWS3] = o3[rows3]
        values = jnp.concatenate([value4[rows4], value3[rows3]], axis=0)
        line = jnp.sum(jnp.where(row == col, values, 0.0), axis=0, keepdims=True)
        high = line.astype(BF16).astype(F32)
        middle = (line - high).astype(BF16).astype(F32)
        low = line - high - middle
        three = jnp.where(
            term == 0, high, jnp.where(term == 1, middle, jnp.where(term == 2, low, 0.0))
        )
        back[j, ROWS4 + ROWS3 :] = three.astype(BF16)


def merge_body(s, fine, two, two_back, row_back, mine, send):
    low = (1 - s[1]) * HEADS
    row = lax.broadcasted_iota(jnp.int32, (ROWS4 + ROWS3, 128), 0)
    lane = lax.broadcasted_iota(jnp.int32, (ROWS4 + ROWS3, 128), 1)

    def joined(first, rows):
        tile = jnp.zeros((ROWS4 + ROWS3, 128), F32)
        for g in range(HEADS):
            three = row_back[first + g, ROWS4 + ROWS3 :].astype(F32)
            line = jnp.sum(three, axis=0, keepdims=True)
            column = jnp.sum(jnp.where(row == lane, line, 0.0), axis=1, keepdims=True)
            tile = jnp.where(lane == g, column, tile)
        o = [row_back[first + g, rows] for g in range(HEADS)]
        return jnp.concatenate(o + [packed_tile(tile[rows])], axis=1)

    four = [joined(side * HEADS, slice(0, ROWS4)) for side in (0, 1)]
    three = joined(low, slice(ROWS4, ROWS4 + ROWS3))
    terms = [
        unpacked(two[...]),
        unpacked(two_back[...]),
        spread(three, 128, 1),
        spread(four[0], 128, 2),
        spread(four[1], 128, 2),
    ]
    outs, weights = merged(terms)
    coarse = jnp.concatenate([o.astype(BF16) for o in outs] + [packed_tile(weights)], axis=1)
    for at, out in enumerate((mine, send)):
        rows = slice(at * B, (at + 1) * B)
        outs, _ = merged(
            [(fine[rows, :COLS], fine[rows, COLS:]), spread(coarse[at * 64 : (at + 1) * 64], B, 2)]
        )
        for h in range(HEADS):
            out[:, h * DH : (h + 1) * DH] = outs[h].astype(BF16)


def join_body(s, mine, theirs, out, sems):
    low = pl.multiple_of(s[0] * COLS, COLS)
    high = pl.multiple_of((1 - s[0]) * COLS, COLS)
    copies = [
        pltpu.make_async_copy(mine, out.at[:, pl.ds(low, COLS)], sems.at[0]),
        pltpu.make_async_copy(theirs, out.at[:, pl.ds(high, COLS)], sems.at[1]),
    ]
    for copy in copies:
        copy.start()
    for copy in copies:
        copy.wait()


def join(s, mine, theirs):
    return pl.pallas_call(
        join_body,
        out_shape=shaped(B, 2 * COLS),
        in_specs=[pl.BlockSpec(memory_space=pltpu.SMEM)]
        + [pl.BlockSpec(memory_space=pltpu.VMEM)] * 2,
        out_specs=pl.BlockSpec(memory_space=pl.ANY),
        scratch_shapes=[pltpu.SemaphoreType.DMA((2,))],
        compiler_params=pltpu.CompilerParams(vmem_limit_bytes=VMEM_LIMIT),
    )(s, mine, theirs)


def pairs_of(target):
    pairs = []
    for chip in range(CHIPS):
        to = target(chip)
        if 0 <= to < CHIPS:
            pairs += [(2 * chip + core, 2 * to + core) for core in (0, 1)]
    return pairs


SWAP = [(i, i ^ 1) for i in range(2 * CHIPS)]
RIGHT = pairs_of(lambda chip: chip + 1)
LEFT = pairs_of(lambda chip: chip - 1)
PAIR = pairs_of(lambda chip: chip ^ 1)
BOUND = pairs_of(lambda chip: chip + 1 if chip % 2 else chip - 1)
ROW = pairs_of(lambda chip: chip - RING if chip % RING < RING // 2 else chip + RING)
LINES = [
    [2 * (row * RING + z) + core for z in range(RING)]
    for row in range(CHIPS // RING)
    for core in (0, 1)
]


def send_to(x, pairs):
    return lax.ppermute(x, "seq", pairs)


def after(x, y):
    return lax.optimization_barrier((x, y))


def line_swap(x):
    return lax.all_to_all(x, "seq", 0, 0, axis_index_groups=LINES)


def local(query_rows, key_rows, value_rows):
    position = lax.axis_index("seq")
    core = position % 2
    chip = position // 2
    z = chip % RING
    row = chip // RING
    half = z // HEADS
    odd = chip % 2
    has_left = chip >= 1
    has_right = chip <= CHIPS - 2
    has_pair = jnp.where(odd == 1, chip <= CHIPS - 3, chip >= 2)
    has_row = jnp.where(half == 1, row >= 1, row <= CHIPS // RING - 2)
    s = jnp.stack(
        [core, half, has_left, has_right, has_pair, z % HEADS, has_row, odd]
    ).astype(jnp.int32)

    own = half_columns(s, (query_rows, key_rows, value_rows))
    q1, k1, v1 = [send_to(x, SWAP) for x in (query_rows, key_rows, value_rows)]
    (apay,) = call(pool_body, (shaped(RING, SEND, DH),), s, (own, q1, k1, v1), wide=(1, 2, 3))
    ain = line_swap(apay)
    s, _ = after(s, apay)
    pay = shaped(3 * B, COLS)
    rpay, lpay = call(
        edge_body,
        (pay, pay),
        s,
        (own, k1, v1),
        wide=(1, 2),
        extra=[pltpu.VMEM(pay.shape, BF16)] * 2 + [pltpu.SemaphoreType.DMA((2,))],
        slow=True,
    )
    rin = send_to(rpay, RIGHT)
    lin = send_to(lpay, LEFT)
    s, _ = after(s, (rpay, lpay))
    (xpay,) = call(row_pay_body, (shaped(4 * B, DH),), s, (ain,))
    xin = send_to(xpay, ROW)
    s, _ = after(s, xpay)
    (near,) = call(near_body, (shaped(2 * B, PACK),), s, (own, q1, k1, v1), wide=(1, 2, 3))
    (q_two,) = call(pair_pay_body, (shaped(128, COLS),), s, (own, q1), wide=(1,))
    pin = send_to(q_two, PAIR)
    s, _ = after(s, (near, q_two))
    (back,) = call(row_body, (shaped(RING, BACK, DH),), s, (ain, xin))
    row_back = line_swap(back)
    s, _ = after(s, back)
    (bpay,) = call(derive_body, (shaped(B, COLS),), s, (rin, lin))
    bin_ = send_to(bpay, BOUND)
    s, _ = after(s, bpay)
    (far,) = call(far_body, (shaped(2 * B, PACK),), s, (own, q1, rin, lin), wide=(1,))
    s, _ = after(s, (far, row_back))
    two, theirs = call(
        pair_body, (shaped(128, PACK), shaped(128, PACK)), s, (q_two, rin, lin, pin, bin_)
    )
    two_back = send_to(theirs, PAIR)
    s, _ = after(s, theirs)
    (fine,) = call(
        one_body,
        (jax.ShapeDtypeStruct((2 * B, PACK), F32),),
        s,
        (own, q1, near, far, rin, lin),
        wide=(1,),
        extra=[pltpu.VMEM((B, PACK), BF16)],
    )
    mine, send = call(
        merge_body, (shaped(B, COLS), shaped(B, COLS)), s, (fine, two, two_back, row_back)
    )
    return join(s, mine, send_to(send, SWAP))


def solution(mesh):
    spec = P("seq", None)
    return jax.shard_map(
        local, mesh=mesh, in_specs=(spec, spec, spec), out_specs=spec, check_vma=False
    )
```

```python
import functools
import math

import jax
import jax.numpy as jnp
from jax import lax
from jax.experimental import pallas as pl
from jax.experimental.pallas import tpu as pltpu
from jax.sharding import PartitionSpec as P

HEADS = 4
DH = 128
COLS = HEADS * DH
B = 256
PACK = COLS + 128
ABSENT = -1e30
SCALE = math.log2(math.e) / math.sqrt(DH)
F32 = jnp.float32
BF16 = jnp.bfloat16

CHIPS = 128
RING = 8
ROWS4, ROWS3 = 32, 64
SEND = 3 * ROWS4 + 2 * ROWS3
BACK = ROWS4 + ROWS3 + 16
VMEM_LIMIT = 10 * 2**20
EDGE = 3 * B


def shaped(*shape):
    return jax.ShapeDtypeStruct(shape, BF16)


def call(body, outs, scalars, arrays, wide=(), extra=(), slow=False):
    def outer(s, *refs):
        start = pl.multiple_of(s[0] * COLS, COLS)
        refs = [
            ref.at[:, pl.ds(start, COLS)] if i in wide else ref for i, ref in enumerate(refs)
        ]
        body(s, *refs)

    return pl.pallas_call(
        outer,
        out_shape=[pltpu.HBM(o.shape, o.dtype) for o in outs] if slow else outs,
        in_specs=[pl.BlockSpec(memory_space=pltpu.SMEM)]
        + [pl.BlockSpec(memory_space=pltpu.VMEM)] * len(arrays),
        out_specs=[pl.BlockSpec(memory_space=pltpu.HBM if slow else pltpu.VMEM)] * len(outs),
        scratch_shapes=list(extra),
        compiler_params=pltpu.CompilerParams(vmem_limit_bytes=VMEM_LIMIT),
        cost_estimate=pl.CostEstimate(flops=0, bytes_accessed=0, transcendentals=0),
    )(scalars, *arrays)


def half_body(s, q, k, v, out, sems):
    start = pl.multiple_of(s[0] * COLS, COLS)
    copies = [
        pltpu.make_async_copy(ref.at[:, pl.ds(start, COLS)], out.at[i], sems.at[i])
        for i, ref in enumerate((q, k, v))
    ]
    for copy in copies:
        copy.start()
    for copy in copies:
        copy.wait()


def half_columns(s, arrays):
    return pl.pallas_call(
        half_body,
        out_shape=shaped(3, B, COLS),
        in_specs=[pl.BlockSpec(memory_space=pltpu.SMEM)]
        + [pl.BlockSpec(memory_space=pltpu.HBM)] * 3,
        out_specs=pl.BlockSpec(memory_space=pltpu.VMEM),
        scratch_shapes=[pltpu.SemaphoreType.DMA((3,))],
        compiler_params=pltpu.CompilerParams(vmem_limit_bytes=VMEM_LIMIT),
        cost_estimate=pl.CostEstimate(flops=0, bytes_accessed=0, transcendentals=0),
    )(s, *(pltpu.with_memory_space_constraint(x, pltpu.HBM) for x in arrays))


def pool_matrix(rows, width, level, scale):
    row = lax.broadcasted_iota(jnp.int32, (rows, width), 0)
    col = lax.broadcasted_iota(jnp.int32, (rows, width), 1)
    return jnp.where((col >> level) == row, scale, 0.0).astype(BF16)


def spread_matrix(rows, width, level):
    row = lax.broadcasted_iota(jnp.int32, (rows, width), 0)
    col = lax.broadcasted_iota(jnp.int32, (rows, width), 1)
    return jnp.where((row >> level) == col, 1.0, 0.0).astype(BF16)


def pooled(x, level, mean):
    rows = x.shape[0]
    scale = 1.0 / 2**level if mean else 1.0
    matrix = pool_matrix(rows >> level, rows, level, scale)
    return jnp.dot(matrix, x, preferred_element_type=F32).astype(BF16)


def attend(jobs, factor):
    results = []
    scores = []
    for q, parts in jobs:
        row = []
        for k, _, bias in parts:
            s = lax.dot_general(q, k, (((1,), (1,)), ((), ())), preferred_element_type=F32) * SCALE
            row.append(s if bias is None else s + bias)
        scores.append(row)
    tops = [
        functools.reduce(jnp.maximum, [jnp.max(s, axis=1, keepdims=True) for s in row])
        for row in scores
    ]
    weights = [[jnp.exp2(s - m) for s in row] for row, m in zip(scores, tops)]
    totals = [
        functools.reduce(jnp.add, [jnp.sum(w, axis=1, keepdims=True) for w in row]) * factor
        for row in weights
    ]
    for (_, parts), row, m, total in zip(jobs, weights, tops, totals):
        out = None
        for w, (_, v, _) in zip(row, parts):
            o = jnp.dot(w.astype(BF16), v, preferred_element_type=F32)
            out = o if out is None else out + o
        results.append(((out / total).astype(BF16), m + jnp.log2(total)))
    return results


def tile_of(values):
    rows = values[0].shape[0]
    lane = lax.broadcasted_iota(jnp.int32, (rows, 128), 1)
    full = jnp.zeros((rows, 128), F32)
    for h, value in enumerate(values):
        full = jnp.where((lane & 3) == h, value, full)
    high = full.astype(BF16)
    rest = full - high.astype(F32)
    middle = rest.astype(BF16)
    low = (rest - middle.astype(F32)).astype(BF16)
    zero = jnp.zeros((rows, 128), BF16)
    part = lane >> 2
    return jnp.where(part == 0, high, jnp.where(part == 1, middle, jnp.where(part == 2, low, zero)))


def merged(terms):
    top = functools.reduce(jnp.maximum, [t for _, t in terms])
    weights = [jnp.exp2(t - top) for _, t in terms]
    total = functools.reduce(jnp.add, weights)
    inverse = 1.0 / total
    weights = [t * inverse for t in weights]
    outs = []
    for h in range(HEADS):
        cols = slice(h * DH, (h + 1) * DH)
        parts = [o[:, cols] * t[:, h : h + 1] for (o, _), t in zip(terms, weights)]
        outs.append(functools.reduce(jnp.add, parts))
    return outs, top + jnp.log2(total)


def unpacked(values):
    values = values.astype(F32)
    t = values[:, COLS:]
    return values[:, :COLS], t + pltpu.roll(t, 128 - 4, 1) + pltpu.roll(t, 128 - 8, 1)


def packed_tile(full):
    lane = lax.broadcasted_iota(jnp.int32, full.shape, 1)
    full = jnp.where(lane < HEADS, full, 0.0)
    high = full.astype(BF16).astype(F32)
    middle = (full - high).astype(BF16).astype(F32)
    low = (full - high - middle).astype(BF16).astype(F32)
    return (high + pltpu.roll(middle, 4, 1) + pltpu.roll(low, 8, 1)).astype(BF16)


def spread(values, rows, level):
    matrix = spread_matrix(rows, rows >> level, level)
    return unpacked(jnp.dot(matrix, values, preferred_element_type=F32))


def attend_to(out_ref, row, q_of, parts_of, rows, factor, group=2):
    values = []
    for first in range(0, HEADS, group):
        spans = [slice(h * DH, (h + 1) * DH) for h in range(first, first + group)]
        for cols, (o, value) in zip(
            spans, attend([(q_of(cols), parts_of(cols)) for cols in spans], factor)
        ):
            out_ref[row : row + rows, cols] = o
            values.append(value)
    out_ref[row : row + rows, COLS:PACK] = tile_of(values)


def edge_body(s, own, q1, k1, v1, rout, lout, rpay, lpay, sems):
    copies = []
    for i, (pay, out) in enumerate(((rpay, rout), (lpay, lout))):
        first = s[0] == 1 - i
        for n, ref in enumerate((k1, v1)):
            mine, other = own[1 + n], ref[...]
            pay[n * B : (n + 1) * B] = jnp.where(first, mine, other)
            pay[2 * B + n * 128 : 2 * B + (n + 1) * 128] = pooled(
                jnp.where(first, other, mine), 1, n == 0
            )
        for n, x in enumerate((own[0], q1[...])):
            pay[EDGE + n * 64 : EDGE + (n + 1) * 64] = pooled(x, 2, True)
        copies.append(pltpu.make_async_copy(pay, out, sems.at[i]))
        copies[-1].start()
    for copy in copies:
        copy.wait()


def pool_body(s, own, q1, k1, v1, apay):
    half = s[1]
    for at in (0, 1):
        whole = (own[0], own[1], own[2]) if at == 0 else (q1[...], k1[...], v1[...])
        three = [pooled(x, 3, n < 2) for n, x in enumerate(whole)]
        four = [pooled(x, 4, n < 2) for n, x in enumerate(whole)]
        for j in range(RING):
            cols = slice((j % HEADS) * DH, (j % HEADS + 1) * DH)
            for n in range(3):
                apay[j, n * ROWS4 + at * 16 : n * ROWS4 + (at + 1) * 16] = four[n][:, cols]
            first = jnp.where(half == j // HEADS, three[1][:, cols], three[0][:, cols])
            base = 3 * ROWS4
            apay[j, base + at * 32 : base + (at + 1) * 32] = first
            base += ROWS3
            apay[j, base + at * 32 : base + (at + 1) * 32] = three[2][:, cols]


def near_body(s, own, q1, k1, v1, out):
    k0, v0 = own.at[1], own.at[2]
    for at, q in enumerate((own.at[0], q1)):
        rows = slice(at * B, (at + 1) * B)
        out[rows, PACK:] = q[...]
        attend_to(
            out,
            at * B,
            lambda cols: q[:, cols],
            lambda cols: [(k0[:, cols], v0[:, cols], None), (k1[:, cols], v1[:, cols], None)],
            B,
            1.0,
        )


def level_two(ref, n):
    near = pooled(ref[n * B : (n + 1) * B], 2, n == 0)
    far = pooled(ref[2 * B + n * 128 : 2 * B + (n + 1) * 128], 1, n == 0)
    return jnp.concatenate([near, far], axis=0)


def block_body(s, own, k1, v1, bpay):
    for n, ref in enumerate((k1, v1)):
        bpay[n * 128 : n * 128 + 64] = pooled(own[1 + n], 2, n == 0)
        bpay[n * 128 + 64 : (n + 1) * 128] = pooled(ref[...], 2, n == 0)


def sides(s):
    left = jnp.where(s[2] == 1, 0.0, ABSENT).astype(F32)
    right = jnp.where(s[3] == 1, 0.0, ABSENT).astype(F32)
    return left, right


def far_body(s, near, rin, lin, out, far):
    first = s[0] == 0
    bias_left, bias_right = sides(s)
    for at in (0, 1):
        rows = slice(at * B, (at + 1) * B)
        left = first if at == 0 else jnp.logical_not(first)
        bias = jnp.where(left, bias_left, bias_right)
        attend_to(
            far,
            at * B,
            lambda cols: near[rows, PACK + cols.start : PACK + cols.stop],
            lambda cols: [
                (
                    jnp.where(left, rin[:B, cols], lin[:B, cols]),
                    jnp.where(left, rin[B : 2 * B, cols], lin[B : 2 * B, cols]),
                    bias,
                )
            ],
            B,
            1.0,
        )
        outs, weights = merged([unpacked(near[rows, :PACK]), unpacked(far[rows])])
        for h in range(HEADS):
            out[rows, h * DH : (h + 1) * DH] = outs[h].astype(BF16)
        out[rows, COLS:PACK] = packed_tile(weights)
        out[at * 128 : (at + 1) * 128, PACK:] = pooled(near[rows, PACK:], 1, True)


def one_body(s, far, rin, lin, out, one):
    def coarse(cols):
        parts = []
        for ref, bias in zip((rin, lin), sides(s)):
            keys = pooled(ref[:B, cols], 1, True)
            values = pooled(ref[B : 2 * B, cols], 1, False)
            keys = jnp.concatenate([keys, ref[2 * B : 2 * B + 128, cols]], axis=0)
            values = jnp.concatenate([values, ref[2 * B + 128 : EDGE, cols]], axis=0)
            parts.append((keys, values, bias))
        return parts

    attend_to(
        one, 0, lambda cols: far[:B, PACK + cols.start : PACK + cols.stop], coarse, B, 2.0
    )
    for at in (0, 1):
        rows = slice(at * B, (at + 1) * B)
        level_one = spread(one[at * 128 : (at + 1) * 128], B, 1)
        outs, weights = merged([unpacked(far[rows, :PACK]), level_one])
        for h in range(HEADS):
            out[rows, h * DH : (h + 1) * DH] = outs[h]
        out[rows, COLS:] = weights


def pair_body(s, near, rin, lin, bin_, mine, theirs):
    bias = jnp.where(s[4] == 1, 0.0, ABSENT).astype(F32)
    odd = s[7] == 1
    kept = [
        jnp.concatenate(
            [
                jnp.where(odd, level_two(lin, n), level_two(rin, n)),
                bin_[n * 128 : (n + 1) * 128],
            ],
            axis=0,
        )
        for n in (0, 1)
    ]
    own_two = jnp.concatenate([pooled(near[at * B : (at + 1) * B, PACK:], 2, True) for at in (0, 1)])
    partner = jnp.where(odd, rin[EDGE:], lin[EDGE:])
    for out, ref in ((theirs, partner), (mine, own_two)):
        attend_to(
            out,
            0,
            lambda cols: ref[:, cols],
            lambda cols: [(kept[0][:, cols], kept[1][:, cols], bias)],
            128,
            4.0,
            4,
        )


def row_pay_body(s, ain, xpay):
    same = s[1] * HEADS
    for j in range(RING):
        xpay[j * ROWS4 : (j + 1) * ROWS4] = ain[j, ROWS4 : 2 * ROWS4]
        xpay[B + j * ROWS4 : B + (j + 1) * ROWS4] = ain[j, 2 * ROWS4 : 3 * ROWS4]
    for j in range(HEADS):
        for n in (0, 1):
            base = 3 * ROWS4 + n * ROWS3
            to = (2 + n) * B + j * ROWS3
            xpay[to : to + ROWS3] = ain[same + j, base : base + ROWS3]


def row_body(s, ain, xin, back):
    half, head = s[1], s[5]
    bias = jnp.where(s[6] == 1, 0.0, ABSENT).astype(F32)
    mine, other = half * HEADS, (1 - half) * HEADS
    base = 3 * ROWS4
    rows3 = lambda at, low: jnp.concatenate(
        [ain[at + j, low : low + ROWS3] for j in range(HEADS)], axis=0
    )
    q4 = jnp.concatenate([ain[j, :ROWS4] for j in range(RING)], axis=0)
    ((o4, value4),) = attend([(q4, [(xin[:B], xin[B : 2 * B], bias)])], 16.0)
    parts = [
        (rows3(mine, base), rows3(mine, base + ROWS3), None),
        (xin[2 * B : 3 * B], xin[3 * B :], bias),
    ]
    ((o3, value3),) = attend([(rows3(other, base), parts)], 8.0)
    row = lax.broadcasted_iota(jnp.int32, (ROWS4 + ROWS3, 128), 0)
    col = lax.broadcasted_iota(jnp.int32, (ROWS4 + ROWS3, 128), 1)
    term = lax.broadcasted_iota(jnp.int32, (16, 128), 0)
    for j in range(RING):
        rows4 = slice(j * ROWS4, (j + 1) * ROWS4)
        rows3 = slice((j % HEADS) * ROWS3, (j % HEADS + 1) * ROWS3)
        back[j, :ROWS4] = o4[rows4]
        back[j, ROWS4 : ROWS4 + ROWS3] = o3[rows3]
        values = jnp.concatenate([value4[rows4], value3[rows3]], axis=0)
        line = jnp.sum(jnp.where(row == col, values, 0.0), axis=0, keepdims=True)
        high = line.astype(BF16).astype(F32)
        middle = (line - high).astype(BF16).astype(F32)
        low = line - high - middle
        three = jnp.where(
            term == 0, high, jnp.where(term == 1, middle, jnp.where(term == 2, low, 0.0))
        )
        back[j, ROWS4 + ROWS3 :] = three.astype(BF16)


def merge_body(s, fine, two, two_back, row_back, mine, send):
    low = (1 - s[1]) * HEADS
    row = lax.broadcasted_iota(jnp.int32, (ROWS4 + ROWS3, 128), 0)
    lane = lax.broadcasted_iota(jnp.int32, (ROWS4 + ROWS3, 128), 1)

    def joined(first, rows):
        tile = jnp.zeros((ROWS4 + ROWS3, 128), F32)
        for g in range(HEADS):
            three = row_back[first + g, ROWS4 + ROWS3 :].astype(F32)
            line = jnp.sum(three, axis=0, keepdims=True)
            column = jnp.sum(jnp.where(row == lane, line, 0.0), axis=1, keepdims=True)
            tile = jnp.where(lane == g, column, tile)
        o = [row_back[first + g, rows] for g in range(HEADS)]
        return jnp.concatenate(o + [packed_tile(tile[rows])], axis=1)

    four = [joined(side * HEADS, slice(0, ROWS4)) for side in (0, 1)]
    three = joined(low, slice(ROWS4, ROWS4 + ROWS3))
    terms = [
        unpacked(two[...]),
        unpacked(two_back[...]),
        spread(three, 128, 1),
        spread(four[0], 128, 2),
        spread(four[1], 128, 2),
    ]
    outs, weights = merged(terms)
    coarse = jnp.concatenate([o.astype(BF16) for o in outs] + [packed_tile(weights)], axis=1)
    for at, out in enumerate((mine, send)):
        rows = slice(at * B, (at + 1) * B)
        outs, _ = merged(
            [(fine[rows, :COLS], fine[rows, COLS:]), spread(coarse[at * 64 : (at + 1) * 64], B, 2)]
        )
        for h in range(HEADS):
            out[:, h * DH : (h + 1) * DH] = outs[h].astype(BF16)


def join_body(s, mine, theirs, out, sems):
    low = pl.multiple_of(s[0] * COLS, COLS)
    high = pl.multiple_of((1 - s[0]) * COLS, COLS)
    copies = [
        pltpu.make_async_copy(mine, out.at[:, pl.ds(low, COLS)], sems.at[0]),
        pltpu.make_async_copy(theirs, out.at[:, pl.ds(high, COLS)], sems.at[1]),
    ]
    for copy in copies:
        copy.start()
    for copy in copies:
        copy.wait()


def join(s, mine, theirs):
    return pl.pallas_call(
        join_body,
        out_shape=shaped(B, 2 * COLS),
        in_specs=[pl.BlockSpec(memory_space=pltpu.SMEM)]
        + [pl.BlockSpec(memory_space=pltpu.VMEM)] * 2,
        out_specs=pl.BlockSpec(memory_space=pl.ANY),
        scratch_shapes=[pltpu.SemaphoreType.DMA((2,))],
        compiler_params=pltpu.CompilerParams(vmem_limit_bytes=VMEM_LIMIT),
    )(s, mine, theirs)


def pairs_of(target):
    pairs = []
    for chip in range(CHIPS):
        to = target(chip)
        if 0 <= to < CHIPS:
            pairs += [(2 * chip + core, 2 * to + core) for core in (0, 1)]
    return pairs


SWAP = [(i, i ^ 1) for i in range(2 * CHIPS)]
RIGHT = pairs_of(lambda chip: chip + 1)
LEFT = pairs_of(lambda chip: chip - 1)
PAIR = pairs_of(lambda chip: chip ^ 1)
BOUND = pairs_of(lambda chip: chip - 2 if chip % 2 else chip + 2)
ROW = pairs_of(lambda chip: chip - RING if chip % RING < RING // 2 else chip + RING)
LINES = [
    [2 * (row * RING + z) + core for z in range(RING)]
    for row in range(CHIPS // RING)
    for core in (0, 1)
]


def send_to(x, pairs):
    return lax.ppermute(x, "seq", pairs)


def after(x, y):
    return lax.optimization_barrier((x, y))


def line_swap(x):
    return lax.all_to_all(x, "seq", 0, 0, axis_index_groups=LINES)


def local(query_rows, key_rows, value_rows):
    position = lax.axis_index("seq")
    core = position % 2
    chip = position // 2
    z = chip % RING
    row = chip // RING
    half = z // HEADS
    odd = chip % 2
    has_left = chip >= 1
    has_right = chip <= CHIPS - 2
    has_pair = jnp.where(odd == 1, chip <= CHIPS - 3, chip >= 2)
    has_row = jnp.where(half == 1, row >= 1, row <= CHIPS // RING - 2)
    s = jnp.stack(
        [core, half, has_left, has_right, has_pair, z % HEADS, has_row, odd]
    ).astype(jnp.int32)

    own = half_columns(s, (query_rows, key_rows, value_rows))
    q1, k1, v1 = [send_to(x, SWAP) for x in (query_rows, key_rows, value_rows)]
    (apay,) = call(pool_body, (shaped(RING, SEND, DH),), s, (own, q1, k1, v1), wide=(1, 2, 3))
    ain = line_swap(apay)
    s, _ = after(s, apay)
    pay = shaped(EDGE + 128, COLS)
    rpay, lpay = call(
        edge_body,
        (pay, pay),
        s,
        (own, q1, k1, v1),
        wide=(1, 2, 3),
        extra=[pltpu.VMEM(pay.shape, BF16)] * 2 + [pltpu.SemaphoreType.DMA((2,))],
        slow=True,
    )
    rin = send_to(rpay, RIGHT)
    lin = send_to(lpay, LEFT)
    s, _ = after(s, (rpay, lpay))
    (xpay,) = call(row_pay_body, (shaped(4 * B, DH),), s, (ain,))
    xin = send_to(xpay, ROW)
    s, _ = after(s, xpay)
    (bpay,) = call(block_body, (shaped(B, COLS),), s, (own, k1, v1), wide=(1, 2))
    bin_ = send_to(bpay, BOUND)
    s, _ = after(s, bpay)
    (near,) = call(
        near_body,
        (shaped(2 * B, PACK + COLS),),
        s,
        (own, q1, k1, v1),
        wide=(1, 2, 3),
    )
    s, _ = after(s, near)
    (back,) = call(row_body, (shaped(RING, BACK, DH),), s, (ain, xin))
    row_back = line_swap(back)
    s, _ = after(s, back)
    (far,) = call(
        far_body,
        (shaped(2 * B, PACK + COLS),),
        s,
        (near, rin, lin),
        extra=[pltpu.VMEM((2 * B, PACK), BF16)],
    )
    s, _ = after(s, far)
    two, theirs = call(
        pair_body, (shaped(128, PACK), shaped(128, PACK)), s, (near, rin, lin, bin_)
    )
    two_back = send_to(theirs, PAIR)
    s, _ = after(s, theirs)
    (fine,) = call(
        one_body,
        (jax.ShapeDtypeStruct((2 * B, PACK), F32),),
        s,
        (far, rin, lin),
        extra=[pltpu.VMEM((B, PACK), BF16)],
    )
    mine, send = call(
        merge_body, (shaped(B, COLS), shaped(B, COLS)), s, (fine, two, two_back, row_back)
    )
    return join(s, mine, send_to(send, SWAP))


def solution(mesh):
    spec = P("seq", None)
    return jax.shard_map(
        local, mesh=mesh, in_specs=(spec, spec, spec), out_specs=spec, check_vma=False
    )
```

```python
import functools
import math

import jax
import jax.numpy as jnp
from jax import lax
from jax.experimental import pallas as pl
from jax.experimental.pallas import tpu as pltpu
from jax.sharding import PartitionSpec as P

HEADS = 4
DH = 128
COLS = HEADS * DH
B = 256
PACK = COLS + 128
ABSENT = -1e30
SCALE = math.log2(math.e) / math.sqrt(DH)
F32 = jnp.float32
BF16 = jnp.bfloat16

CHIPS = 128
RING = 8
ROWS4, ROWS3 = 32, 64
SEND = 3 * ROWS4 + 2 * ROWS3
BACK = ROWS4 + ROWS3 + 16
VMEM_LIMIT = 10 * 2**20
EDGE = 3 * B


def shaped(*shape):
    return jax.ShapeDtypeStruct(shape, BF16)


def call(body, outs, scalars, arrays, wide=(), extra=(), slow=False):
    def outer(s, *refs):
        start = pl.multiple_of(s[0] * COLS, COLS)
        refs = [
            ref.at[:, pl.ds(start, COLS)] if i in wide else ref for i, ref in enumerate(refs)
        ]
        body(s, *refs)

    return pl.pallas_call(
        outer,
        out_shape=[pltpu.HBM(o.shape, o.dtype) for o in outs] if slow else outs,
        in_specs=[pl.BlockSpec(memory_space=pltpu.SMEM)]
        + [pl.BlockSpec(memory_space=pltpu.VMEM)] * len(arrays),
        out_specs=[pl.BlockSpec(memory_space=pltpu.HBM if slow else pltpu.VMEM)] * len(outs),
        scratch_shapes=list(extra),
        compiler_params=pltpu.CompilerParams(vmem_limit_bytes=VMEM_LIMIT),
        cost_estimate=pl.CostEstimate(flops=0, bytes_accessed=0, transcendentals=0),
    )(scalars, *arrays)


def half_body(s, q, k, v, out, sems):
    start = pl.multiple_of(s[0] * COLS, COLS)
    copies = [
        pltpu.make_async_copy(ref.at[:, pl.ds(start, COLS)], out.at[i], sems.at[i])
        for i, ref in enumerate((q, k, v))
    ]
    for copy in copies:
        copy.start()
    for copy in copies:
        copy.wait()


def half_columns(s, arrays):
    return pl.pallas_call(
        half_body,
        out_shape=shaped(3, B, COLS),
        in_specs=[pl.BlockSpec(memory_space=pltpu.SMEM)]
        + [pl.BlockSpec(memory_space=pltpu.HBM)] * 3,
        out_specs=pl.BlockSpec(memory_space=pltpu.VMEM),
        scratch_shapes=[pltpu.SemaphoreType.DMA((3,))],
        compiler_params=pltpu.CompilerParams(vmem_limit_bytes=VMEM_LIMIT),
        cost_estimate=pl.CostEstimate(flops=0, bytes_accessed=0, transcendentals=0),
    )(s, *(pltpu.with_memory_space_constraint(x, pltpu.HBM) for x in arrays))


def pool_matrix(rows, width, level, scale):
    row = lax.broadcasted_iota(jnp.int32, (rows, width), 0)
    col = lax.broadcasted_iota(jnp.int32, (rows, width), 1)
    return jnp.where((col >> level) == row, scale, 0.0).astype(BF16)


def spread_matrix(rows, width, level):
    row = lax.broadcasted_iota(jnp.int32, (rows, width), 0)
    col = lax.broadcasted_iota(jnp.int32, (rows, width), 1)
    return jnp.where((row >> level) == col, 1.0, 0.0).astype(BF16)


def pooled(x, level, mean):
    rows = x.shape[0]
    scale = 1.0 / 2**level if mean else 1.0
    matrix = pool_matrix(rows >> level, rows, level, scale)
    return jnp.dot(matrix, x, preferred_element_type=F32).astype(BF16)


def attend(jobs, factor):
    results = []
    scores = []
    for q, parts in jobs:
        row = []
        for k, _, bias in parts:
            s = lax.dot_general(q, k, (((1,), (1,)), ((), ())), preferred_element_type=F32) * SCALE
            row.append(s if bias is None else s + bias)
        scores.append(row)
    tops = [
        functools.reduce(jnp.maximum, [jnp.max(s, axis=1, keepdims=True) for s in row])
        for row in scores
    ]
    weights = [[jnp.exp2(s - m) for s in row] for row, m in zip(scores, tops)]
    totals = [
        functools.reduce(jnp.add, [jnp.sum(w, axis=1, keepdims=True) for w in row]) * factor
        for row in weights
    ]
    for (_, parts), row, m, total in zip(jobs, weights, tops, totals):
        out = None
        for w, (_, v, _) in zip(row, parts):
            o = jnp.dot(w.astype(BF16), v, preferred_element_type=F32)
            out = o if out is None else out + o
        results.append(((out / total).astype(BF16), m + jnp.log2(total)))
    return results


def tile_of(values):
    rows = values[0].shape[0]
    lane = lax.broadcasted_iota(jnp.int32, (rows, 128), 1)
    full = jnp.zeros((rows, 128), F32)
    for h, value in enumerate(values):
        full = jnp.where((lane & 3) == h, value, full)
    high = full.astype(BF16)
    rest = full - high.astype(F32)
    middle = rest.astype(BF16)
    low = (rest - middle.astype(F32)).astype(BF16)
    zero = jnp.zeros((rows, 128), BF16)
    part = lane >> 2
    return jnp.where(part == 0, high, jnp.where(part == 1, middle, jnp.where(part == 2, low, zero)))


def merged(terms):
    top = functools.reduce(jnp.maximum, [t for _, t in terms])
    weights = [jnp.exp2(t - top) for _, t in terms]
    total = functools.reduce(jnp.add, weights)
    inverse = 1.0 / total
    weights = [t * inverse for t in weights]
    outs = []
    for h in range(HEADS):
        cols = slice(h * DH, (h + 1) * DH)
        parts = [o[:, cols] * t[:, h : h + 1] for (o, _), t in zip(terms, weights)]
        outs.append(functools.reduce(jnp.add, parts))
    return outs, top + jnp.log2(total)


def unpacked(values):
    values = values.astype(F32)
    t = values[:, COLS:]
    return values[:, :COLS], t + pltpu.roll(t, 128 - 4, 1) + pltpu.roll(t, 128 - 8, 1)


def packed_tile(full):
    lane = lax.broadcasted_iota(jnp.int32, full.shape, 1)
    full = jnp.where(lane < HEADS, full, 0.0)
    high = full.astype(BF16).astype(F32)
    middle = (full - high).astype(BF16).astype(F32)
    low = (full - high - middle).astype(BF16).astype(F32)
    return (high + pltpu.roll(middle, 4, 1) + pltpu.roll(low, 8, 1)).astype(BF16)


def spread(values, rows, level):
    matrix = spread_matrix(rows, rows >> level, level)
    return unpacked(jnp.dot(matrix, values, preferred_element_type=F32))


def attend_to(out_ref, row, q_of, parts_of, rows, factor, group=2):
    values = []
    for first in range(0, HEADS, group):
        spans = [slice(h * DH, (h + 1) * DH) for h in range(first, first + group)]
        for cols, (o, value) in zip(
            spans, attend([(q_of(cols), parts_of(cols)) for cols in spans], factor)
        ):
            out_ref[row : row + rows, cols] = o
            values.append(value)
    out_ref[row : row + rows, COLS:PACK] = tile_of(values)


def edge_body(s, own, q1, k1, v1, rout, lout, rpay, lpay, sems):
    copies = []
    queries = [pooled(x, 2, True) for x in (own[0], q1[...])]
    for i, (pay, out) in enumerate(((rpay, rout), (lpay, lout))):
        first = s[0] == 1 - i
        for n, ref in enumerate((k1, v1)):
            mine, other = own[1 + n], ref[...]
            pay[n * B : (n + 1) * B] = jnp.where(first, mine, other)
            pay[2 * B + n * 128 : 2 * B + (n + 1) * 128] = pooled(
                jnp.where(first, other, mine), 1, n == 0
            )
        for n, x in enumerate(queries):
            pay[EDGE + n * 64 : EDGE + (n + 1) * 64] = x
        copies.append(pltpu.make_async_copy(pay, out, sems.at[i]))
        copies[-1].start()
    for copy in copies:
        copy.wait()


def pool_body(s, own, q1, k1, v1, apay):
    half = s[1]
    matrices = [
        jnp.concatenate(
            [pool_matrix(B >> level, B, level, 1.0 / 2**level if mean else 1.0) for level in (3, 4)],
            axis=0,
        )
        for mean in (True, False)
    ]
    for at in (0, 1):
        whole = (own[0], own[1], own[2]) if at == 0 else (q1[...], k1[...], v1[...])
        both = [jnp.dot(matrices[n == 2], x, preferred_element_type=F32) for n, x in enumerate(whole)]
        three = [x[: B >> 3].astype(BF16) for x in both]
        four = [x[B >> 3 :].astype(BF16) for x in both]
        for j in range(RING):
            cols = slice((j % HEADS) * DH, (j % HEADS + 1) * DH)
            for n in range(3):
                apay[j, n * ROWS4 + at * 16 : n * ROWS4 + (at + 1) * 16] = four[n][:, cols]
            first = jnp.where(half == j // HEADS, three[1][:, cols], three[0][:, cols])
            base = 3 * ROWS4
            apay[j, base + at * 32 : base + (at + 1) * 32] = first
            base += ROWS3
            apay[j, base + at * 32 : base + (at + 1) * 32] = three[2][:, cols]


def near_body(s, own, q1, k1, v1, out):
    k0, v0 = own.at[1], own.at[2]
    for at, q in enumerate((own.at[0], q1)):
        rows = slice(at * B, (at + 1) * B)
        out[rows, PACK:] = q[...]
        attend_to(
            out,
            at * B,
            lambda cols: q[:, cols],
            lambda cols: [(k0[:, cols], v0[:, cols], None), (k1[:, cols], v1[:, cols], None)],
            B,
            1.0,
        )


def level_two(x, n):
    near = pooled(x[n * B : (n + 1) * B], 2, n == 0)
    far = pooled(x[2 * B + n * 128 : 2 * B + (n + 1) * 128], 1, n == 0)
    return jnp.concatenate([near, far], axis=0)


def block_body(s, own, k1, v1, bpay):
    for n, ref in enumerate((k1, v1)):
        bpay[n * 128 : n * 128 + 64] = pooled(own[1 + n], 2, n == 0)
        bpay[n * 128 + 64 : (n + 1) * 128] = pooled(ref[...], 2, n == 0)


def sides(s):
    left = jnp.where(s[2] == 1, 0.0, ABSENT).astype(F32)
    right = jnp.where(s[3] == 1, 0.0, ABSENT).astype(F32)
    return left, right


def far_body(s, near, rin, lin, out):
    first = s[0] == 0
    bias_left, bias_right = sides(s)
    for at in (0, 1):
        rows = slice(at * B, (at + 1) * B)
        left = first if at == 0 else jnp.logical_not(first)
        bias = jnp.where(left, bias_left, bias_right)
        attend_to(
            out,
            at * B,
            lambda cols: near[rows, PACK + cols.start : PACK + cols.stop],
            lambda cols: [
                (
                    jnp.where(left, rin[:B, cols], lin[:B, cols]),
                    jnp.where(left, rin[B : 2 * B, cols], lin[B : 2 * B, cols]),
                    bias,
                )
            ],
            B,
            1.0,
        )


def one_body(s, near, far, rin, lin, out, one):
    def coarse(cols):
        parts = []
        for ref, bias in zip((rin, lin), sides(s)):
            keys = pooled(ref[:B, cols], 1, True)
            values = pooled(ref[B : 2 * B, cols], 1, False)
            keys = jnp.concatenate([keys, ref[2 * B : 2 * B + 128, cols]], axis=0)
            values = jnp.concatenate([values, ref[2 * B + 128 : EDGE, cols]], axis=0)
            parts.append((keys, values, bias))
        return parts

    q_one = jnp.concatenate([pooled(near[at * B : (at + 1) * B, PACK:], 1, True) for at in (0, 1)])
    attend_to(one, 0, lambda cols: q_one[:, cols], coarse, B, 2.0)
    for at in (0, 1):
        rows = slice(at * B, (at + 1) * B)
        level_one = spread(one[at * 128 : (at + 1) * 128], B, 1)
        outs, weights = merged([unpacked(near[rows, :PACK]), unpacked(far[rows]), level_one])
        for h in range(HEADS):
            out[rows, h * DH : (h + 1) * DH] = outs[h]
        out[rows, COLS:] = weights


def pair_body(s, near, rin, lin, bin_, mine, theirs):
    bias = jnp.where(s[4] == 1, 0.0, ABSENT).astype(F32)
    odd = s[7] == 1
    beside = jnp.where(odd, lin[:EDGE], rin[:EDGE])
    kept = [
        jnp.concatenate([level_two(beside, n), bin_[n * 128 : (n + 1) * 128]], axis=0)
        for n in (0, 1)
    ]
    queries = [pooled(near[at * B : (at + 1) * B, PACK:], 2, True) for at in (0, 1)]
    queries.append(jnp.where(odd, rin[EDGE:], lin[EDGE:]))
    queries = jnp.concatenate(queries, axis=0)
    spans = [slice(h * DH, (h + 1) * DH) for h in range(HEADS)]
    jobs = [(queries[:, cols], [(kept[0][:, cols], kept[1][:, cols], bias)]) for cols in spans]
    values = []
    for cols, (o, value) in zip(spans, attend(jobs, 4.0)):
        mine[:, cols] = o[:128]
        theirs[:, cols] = o[128:]
        values.append(value)
    tile = tile_of(values)
    mine[:, COLS:] = tile[:128]
    theirs[:, COLS:] = tile[128:]


def row_pay_body(s, ain, xpay):
    same = s[1] * HEADS
    for j in range(RING):
        xpay[j * ROWS4 : (j + 1) * ROWS4] = ain[j, ROWS4 : 2 * ROWS4]
        xpay[B + j * ROWS4 : B + (j + 1) * ROWS4] = ain[j, 2 * ROWS4 : 3 * ROWS4]
    for j in range(HEADS):
        for n in (0, 1):
            base = 3 * ROWS4 + n * ROWS3
            to = (2 + n) * B + j * ROWS3
            xpay[to : to + ROWS3] = ain[same + j, base : base + ROWS3]


def row_body(s, ain, xin, back):
    half, head = s[1], s[5]
    bias = jnp.where(s[6] == 1, 0.0, ABSENT).astype(F32)
    mine, other = half * HEADS, (1 - half) * HEADS
    base = 3 * ROWS4
    rows3 = lambda at, low: jnp.concatenate(
        [ain[at + j, low : low + ROWS3] for j in range(HEADS)], axis=0
    )
    q4 = jnp.concatenate([ain[j, :ROWS4] for j in range(RING)], axis=0)
    ((o4, value4),) = attend([(q4, [(xin[:B], xin[B : 2 * B], bias)])], 16.0)
    parts = [
        (rows3(mine, base), rows3(mine, base + ROWS3), None),
        (xin[2 * B : 3 * B], xin[3 * B :], bias),
    ]
    ((o3, value3),) = attend([(rows3(other, base), parts)], 8.0)
    row = lax.broadcasted_iota(jnp.int32, (ROWS4 + ROWS3, 128), 0)
    col = lax.broadcasted_iota(jnp.int32, (ROWS4 + ROWS3, 128), 1)
    term = lax.broadcasted_iota(jnp.int32, (16, 128), 0)
    for j in range(RING):
        rows4 = slice(j * ROWS4, (j + 1) * ROWS4)
        rows3 = slice((j % HEADS) * ROWS3, (j % HEADS + 1) * ROWS3)
        back[j, :ROWS4] = o4[rows4]
        back[j, ROWS4 : ROWS4 + ROWS3] = o3[rows3]
        values = jnp.concatenate([value4[rows4], value3[rows3]], axis=0)
        line = jnp.sum(jnp.where(row == col, values, 0.0), axis=0, keepdims=True)
        high = line.astype(BF16).astype(F32)
        middle = (line - high).astype(BF16).astype(F32)
        low = line - high - middle
        three = jnp.where(
            term == 0, high, jnp.where(term == 1, middle, jnp.where(term == 2, low, 0.0))
        )
        back[j, ROWS4 + ROWS3 :] = three.astype(BF16)


def merge_body(s, fine, two, two_back, row_back, mine, send):
    low = (1 - s[1]) * HEADS
    row = lax.broadcasted_iota(jnp.int32, (ROWS4 + ROWS3, 128), 0)
    lane = lax.broadcasted_iota(jnp.int32, (ROWS4 + ROWS3, 128), 1)

    def joined(first, rows):
        tile = jnp.zeros((ROWS4 + ROWS3, 128), F32)
        for g in range(HEADS):
            three = row_back[first + g, ROWS4 + ROWS3 :].astype(F32)
            line = jnp.sum(three, axis=0, keepdims=True)
            column = jnp.sum(jnp.where(row == lane, line, 0.0), axis=1, keepdims=True)
            tile = jnp.where(lane == g, column, tile)
        o = [row_back[first + g, rows] for g in range(HEADS)]
        return jnp.concatenate(o + [packed_tile(tile[rows])], axis=1)

    four = [joined(side * HEADS, slice(0, ROWS4)) for side in (0, 1)]
    three = joined(low, slice(ROWS4, ROWS4 + ROWS3))
    terms = [
        unpacked(two[...]),
        unpacked(two_back[...]),
        spread(three, 128, 1),
        spread(four[0], 128, 2),
        spread(four[1], 128, 2),
    ]
    outs, weights = merged(terms)
    coarse = jnp.concatenate([o.astype(BF16) for o in outs] + [packed_tile(weights)], axis=1)
    for at, out in enumerate((mine, send)):
        rows = slice(at * B, (at + 1) * B)
        outs, _ = merged(
            [(fine[rows, :COLS], fine[rows, COLS:]), spread(coarse[at * 64 : (at + 1) * 64], B, 2)]
        )
        for h in range(HEADS):
            out[:, h * DH : (h + 1) * DH] = outs[h].astype(BF16)


def join_body(s, mine, theirs, out, sems):
    low = pl.multiple_of(s[0] * COLS, COLS)
    high = pl.multiple_of((1 - s[0]) * COLS, COLS)
    copies = [
        pltpu.make_async_copy(mine, out.at[:, pl.ds(low, COLS)], sems.at[0]),
        pltpu.make_async_copy(theirs, out.at[:, pl.ds(high, COLS)], sems.at[1]),
    ]
    for copy in copies:
        copy.start()
    for copy in copies:
        copy.wait()


def join(s, mine, theirs):
    return pl.pallas_call(
        join_body,
        out_shape=shaped(B, 2 * COLS),
        in_specs=[pl.BlockSpec(memory_space=pltpu.SMEM)]
        + [pl.BlockSpec(memory_space=pltpu.VMEM)] * 2,
        out_specs=pl.BlockSpec(memory_space=pl.ANY),
        scratch_shapes=[pltpu.SemaphoreType.DMA((2,))],
        compiler_params=pltpu.CompilerParams(vmem_limit_bytes=VMEM_LIMIT),
    )(s, mine, theirs)


def pairs_of(target):
    pairs = []
    for chip in range(CHIPS):
        to = target(chip)
        if 0 <= to < CHIPS:
            pairs += [(2 * chip + core, 2 * to + core) for core in (0, 1)]
    return pairs


SWAP = [(i, i ^ 1) for i in range(2 * CHIPS)]
RIGHT = pairs_of(lambda chip: chip + 1)
LEFT = pairs_of(lambda chip: chip - 1)
PAIR = pairs_of(lambda chip: chip ^ 1)
BOUND = pairs_of(lambda chip: chip - 2 if chip % 2 else chip + 2)
ROW = pairs_of(lambda chip: chip - RING if chip % RING < RING // 2 else chip + RING)
LINES = [
    [2 * (row * RING + z) + core for z in range(RING)]
    for row in range(CHIPS // RING)
    for core in (0, 1)
]


def send_to(x, pairs):
    return lax.ppermute(x, "seq", pairs)


def after(x, y):
    return lax.optimization_barrier((x, y))


def line_swap(x):
    return lax.all_to_all(x, "seq", 0, 0, axis_index_groups=LINES)


def local(query_rows, key_rows, value_rows):
    position = lax.axis_index("seq")
    core = position % 2
    chip = position // 2
    z = chip % RING
    row = chip // RING
    half = z // HEADS
    odd = chip % 2
    has_left = chip >= 1
    has_right = chip <= CHIPS - 2
    has_pair = jnp.where(odd == 1, chip <= CHIPS - 3, chip >= 2)
    has_row = jnp.where(half == 1, row >= 1, row <= CHIPS // RING - 2)
    s = jnp.stack(
        [core, half, has_left, has_right, has_pair, z % HEADS, has_row, odd]
    ).astype(jnp.int32)

    own = half_columns(s, (query_rows, key_rows, value_rows))
    q1, k1, v1 = [send_to(x, SWAP) for x in (query_rows, key_rows, value_rows)]
    (apay,) = call(pool_body, (shaped(RING, SEND, DH),), s, (own, q1, k1, v1), wide=(1, 2, 3))
    ain = line_swap(apay)
    s, _ = after(s, apay)
    pay = shaped(EDGE + 128, COLS)
    rpay, lpay = call(
        edge_body,
        (pay, pay),
        s,
        (own, q1, k1, v1),
        wide=(1, 2, 3),
        extra=[pltpu.VMEM(pay.shape, BF16)] * 2 + [pltpu.SemaphoreType.DMA((2,))],
        slow=True,
    )
    rin = send_to(rpay, RIGHT)
    lin = send_to(lpay, LEFT)
    s, _ = after(s, (rpay, lpay))
    (xpay,) = call(row_pay_body, (shaped(4 * B, DH),), s, (ain,))
    xin = send_to(xpay, ROW)
    s, _ = after(s, xpay)
    (bpay,) = call(block_body, (shaped(B, COLS),), s, (own, k1, v1), wide=(1, 2))
    bin_ = send_to(bpay, BOUND)
    s, _ = after(s, bpay)
    (near,) = call(
        near_body,
        (shaped(2 * B, PACK + COLS),),
        s,
        (own, q1, k1, v1),
        wide=(1, 2, 3),
    )
    s, _ = after(s, near)
    (back,) = call(row_body, (shaped(RING, BACK, DH),), s, (ain, xin))
    row_back = line_swap(back)
    s, _ = after(s, back)
    (far,) = call(far_body, (shaped(2 * B, PACK),), s, (near, rin, lin))
    s, _ = after(s, far)
    two, theirs = call(
        pair_body, (shaped(128, PACK), shaped(128, PACK)), s, (near, rin, lin, bin_)
    )
    two_back = send_to(theirs, PAIR)
    s, _ = after(s, theirs)
    (fine,) = call(
        one_body,
        (jax.ShapeDtypeStruct((2 * B, PACK), F32),),
        s,
        (near, far, rin, lin),
        extra=[pltpu.VMEM((B, PACK), BF16)],
    )
    mine, send = call(
        merge_body, (shaped(B, COLS), shaped(B, COLS)), s, (fine, two, two_back, row_back)
    )
    return join(s, mine, send_to(send, SWAP))


def solution(mesh):
    spec = P("seq", None)
    return jax.shard_map(
        local, mesh=mesh, in_specs=(spec, spec, spec), out_specs=spec, check_vma=False
    )
```

```python
import functools
import math

import jax
import jax.numpy as jnp
from jax import lax
from jax.experimental import pallas as pl
from jax.experimental.pallas import tpu as pltpu
from jax.sharding import PartitionSpec as P

HEADS = 4
DH = 128
COLS = HEADS * DH
B = 256
PACK = COLS + 128
ABSENT = -1e30
SCALE = math.log2(math.e) / math.sqrt(DH)
F32 = jnp.float32
BF16 = jnp.bfloat16

CHIPS = 128
RING = 8
ROWS4, ROWS3 = 32, 64
SEND = 3 * ROWS4 + 2 * ROWS3
BACK = ROWS4 + ROWS3 + 16
VMEM_LIMIT = 10 * 2**20
EDGE = 3 * B


def shaped(*shape):
    return jax.ShapeDtypeStruct(shape, BF16)


def call(body, outs, scalars, arrays, wide=(), extra=(), slow=False):
    def outer(s, *refs):
        start = pl.multiple_of(s[0] * COLS, COLS)
        refs = [
            ref.at[:, pl.ds(start, COLS)] if i in wide else ref for i, ref in enumerate(refs)
        ]
        body(s, *refs)

    return pl.pallas_call(
        outer,
        out_shape=[pltpu.HBM(o.shape, o.dtype) for o in outs] if slow else outs,
        in_specs=[pl.BlockSpec(memory_space=pltpu.SMEM)]
        + [pl.BlockSpec(memory_space=pltpu.VMEM)] * len(arrays),
        out_specs=[pl.BlockSpec(memory_space=pltpu.HBM if slow else pltpu.VMEM)] * len(outs),
        scratch_shapes=list(extra),
        compiler_params=pltpu.CompilerParams(vmem_limit_bytes=VMEM_LIMIT),
        cost_estimate=pl.CostEstimate(flops=0, bytes_accessed=0, transcendentals=0),
    )(scalars, *arrays)


def half_body(s, q, k, v, out, sems):
    start = pl.multiple_of(s[0] * COLS, COLS)
    copies = [
        pltpu.make_async_copy(ref.at[:, pl.ds(start, COLS)], out.at[i], sems.at[i])
        for i, ref in enumerate((q, k, v))
    ]
    for copy in copies:
        copy.start()
    for copy in copies:
        copy.wait()


def half_columns(s, arrays):
    return pl.pallas_call(
        half_body,
        out_shape=shaped(3, B, COLS),
        in_specs=[pl.BlockSpec(memory_space=pltpu.SMEM)]
        + [pl.BlockSpec(memory_space=pltpu.HBM)] * 3,
        out_specs=pl.BlockSpec(memory_space=pltpu.VMEM),
        scratch_shapes=[pltpu.SemaphoreType.DMA((3,))],
        compiler_params=pltpu.CompilerParams(vmem_limit_bytes=VMEM_LIMIT),
        cost_estimate=pl.CostEstimate(flops=0, bytes_accessed=0, transcendentals=0),
    )(s, *(pltpu.with_memory_space_constraint(x, pltpu.HBM) for x in arrays))


def pool_matrix(rows, width, level, scale):
    row = lax.broadcasted_iota(jnp.int32, (rows, width), 0)
    col = lax.broadcasted_iota(jnp.int32, (rows, width), 1)
    return jnp.where((col >> level) == row, scale, 0.0).astype(BF16)


def spread_matrix(rows, width, level):
    row = lax.broadcasted_iota(jnp.int32, (rows, width), 0)
    col = lax.broadcasted_iota(jnp.int32, (rows, width), 1)
    return jnp.where((row >> level) == col, 1.0, 0.0).astype(BF16)


def pooled(x, level, mean):
    rows = x.shape[0]
    scale = 1.0 / 2**level if mean else 1.0
    matrix = pool_matrix(rows >> level, rows, level, scale)
    return jnp.dot(matrix, x, preferred_element_type=F32).astype(BF16)


def attend(jobs, factor):
    results = []
    scores = []
    for q, parts in jobs:
        row = []
        for k, _, bias in parts:
            s = lax.dot_general(q, k, (((1,), (1,)), ((), ())), preferred_element_type=F32) * SCALE
            row.append(s if bias is None else s + bias)
        scores.append(row)
    tops = [
        functools.reduce(jnp.maximum, [jnp.max(s, axis=1, keepdims=True) for s in row])
        for row in scores
    ]
    weights = [[jnp.exp2(s - m) for s in row] for row, m in zip(scores, tops)]
    totals = [
        functools.reduce(jnp.add, [jnp.sum(w, axis=1, keepdims=True) for w in row]) * factor
        for row in weights
    ]
    for (_, parts), row, m, total in zip(jobs, weights, tops, totals):
        out = None
        for w, (_, v, _) in zip(row, parts):
            o = jnp.dot(w.astype(BF16), v, preferred_element_type=F32)
            out = o if out is None else out + o
        results.append(((out / total).astype(BF16), m + jnp.log2(total)))
    return results


def tile_of(values):
    rows = values[0].shape[0]
    lane = lax.broadcasted_iota(jnp.int32, (rows, 128), 1)
    full = jnp.zeros((rows, 128), F32)
    for h, value in enumerate(values):
        full = jnp.where((lane & 3) == h, value, full)
    high = full.astype(BF16)
    rest = full - high.astype(F32)
    middle = rest.astype(BF16)
    low = (rest - middle.astype(F32)).astype(BF16)
    zero = jnp.zeros((rows, 128), BF16)
    part = lane >> 2
    return jnp.where(part == 0, high, jnp.where(part == 1, middle, jnp.where(part == 2, low, zero)))


def merged(terms):
    top = functools.reduce(jnp.maximum, [t for _, t in terms])
    weights = [jnp.exp2(t - top) for _, t in terms]
    total = functools.reduce(jnp.add, weights)
    inverse = 1.0 / total
    weights = [t * inverse for t in weights]
    outs = []
    for h in range(HEADS):
        cols = slice(h * DH, (h + 1) * DH)
        parts = [o[:, cols] * t[:, h : h + 1] for (o, _), t in zip(terms, weights)]
        outs.append(functools.reduce(jnp.add, parts))
    return outs, top + jnp.log2(total)


def unpacked(values):
    values = values.astype(F32)
    t = values[:, COLS:]
    return values[:, :COLS], t + pltpu.roll(t, 128 - 4, 1) + pltpu.roll(t, 128 - 8, 1)


def packed_tile(full):
    lane = lax.broadcasted_iota(jnp.int32, full.shape, 1)
    full = jnp.where(lane < HEADS, full, 0.0)
    high = full.astype(BF16).astype(F32)
    middle = (full - high).astype(BF16).astype(F32)
    low = (full - high - middle).astype(BF16).astype(F32)
    return (high + pltpu.roll(middle, 4, 1) + pltpu.roll(low, 8, 1)).astype(BF16)


def spread(values, rows, level):
    matrix = spread_matrix(rows, rows >> level, level)
    return unpacked(jnp.dot(matrix, values, preferred_element_type=F32))


def attend_to(out_ref, row, q_of, parts_of, rows, factor, group=2):
    values = []
    for first in range(0, HEADS, group):
        spans = [slice(h * DH, (h + 1) * DH) for h in range(first, first + group)]
        for cols, (o, value) in zip(
            spans, attend([(q_of(cols), parts_of(cols)) for cols in spans], factor)
        ):
            out_ref[row : row + rows, cols] = o
            values.append(value)
    out_ref[row : row + rows, COLS:PACK] = tile_of(values)


def edge_body(s, own, q1, k1, v1, rout, lout, rpay, lpay, sems):
    copies = []
    queries = [pooled(x, 2, True) for x in (own[0], q1[...])]
    for i, (pay, out) in enumerate(((rpay, rout), (lpay, lout))):
        first = s[0] == 1 - i
        for n, ref in enumerate((k1, v1)):
            mine, other = own[1 + n], ref[...]
            pay[n * B : (n + 1) * B] = jnp.where(first, mine, other)
            pay[2 * B + n * 128 : 2 * B + (n + 1) * 128] = pooled(
                jnp.where(first, other, mine), 1, n == 0
            )
        for n, x in enumerate(queries):
            pay[EDGE + n * 64 : EDGE + (n + 1) * 64] = x
        copies.append(pltpu.make_async_copy(pay, out, sems.at[i]))
        copies[-1].start()
    for copy in copies:
        copy.wait()


def pool_body(s, own, q1, k1, v1, apay):
    half = s[1]
    matrices = [
        jnp.concatenate(
            [pool_matrix(B >> level, B, level, 1.0 / 2**level if mean else 1.0) for level in (3, 4)],
            axis=0,
        )
        for mean in (True, False)
    ]
    for at in (0, 1):
        whole = (own[0], own[1], own[2]) if at == 0 else (q1[...], k1[...], v1[...])
        both = [jnp.dot(matrices[n == 2], x, preferred_element_type=F32) for n, x in enumerate(whole)]
        three = [x[: B >> 3].astype(BF16) for x in both]
        four = [x[B >> 3 :].astype(BF16) for x in both]
        for j in range(RING):
            cols = slice((j % HEADS) * DH, (j % HEADS + 1) * DH)
            for n in range(3):
                apay[j, n * ROWS4 + at * 16 : n * ROWS4 + (at + 1) * 16] = four[n][:, cols]
            first = jnp.where(half == j // HEADS, three[1][:, cols], three[0][:, cols])
            base = 3 * ROWS4
            apay[j, base + at * 32 : base + (at + 1) * 32] = first
            base += ROWS3
            apay[j, base + at * 32 : base + (at + 1) * 32] = three[2][:, cols]


def near_body(s, own, q1, k1, v1, out):
    k0, v0 = own.at[1], own.at[2]
    for at, q in enumerate((own.at[0], q1)):
        rows = slice(at * B, (at + 1) * B)
        out[rows, PACK:] = q[...]
        attend_to(
            out,
            at * B,
            lambda cols: q[:, cols],
            lambda cols: [(k0[:, cols], v0[:, cols], None), (k1[:, cols], v1[:, cols], None)],
            B,
            1.0,
        )


def level_two(x, n):
    near = pooled(x[n * B : (n + 1) * B], 2, n == 0)
    far = pooled(x[2 * B + n * 128 : 2 * B + (n + 1) * 128], 1, n == 0)
    return jnp.concatenate([near, far], axis=0)


def block_body(s, own, k1, v1, bpay):
    for n, ref in enumerate((k1, v1)):
        bpay[n * 128 : n * 128 + 64] = pooled(own[1 + n], 2, n == 0)
        bpay[n * 128 + 64 : (n + 1) * 128] = pooled(ref[...], 2, n == 0)


def sides(s):
    left = jnp.where(s[2] == 1, 0.0, ABSENT).astype(F32)
    right = jnp.where(s[3] == 1, 0.0, ABSENT).astype(F32)
    return left, right


def far_body(s, near, rin, lin, out, two_in, one_in):
    first = s[0] == 0
    bias_left, bias_right = sides(s)
    for at in (0, 1):
        rows = slice(at * B, (at + 1) * B)
        left = first if at == 0 else jnp.logical_not(first)
        bias = jnp.where(left, bias_left, bias_right)
        attend_to(
            out,
            at * B,
            lambda cols: near[rows, PACK + cols.start : PACK + cols.stop],
            lambda cols: [
                (
                    jnp.where(left, rin[:B, cols], lin[:B, cols]),
                    jnp.where(left, rin[B : 2 * B, cols], lin[B : 2 * B, cols]),
                    bias,
                )
            ],
            B,
            1.0,
        )


    odd = s[7] == 1
    for at in (0, 1):
        two_in[at * 64 : (at + 1) * 64] = pooled(near[at * B : (at + 1) * B, PACK:], 2, True)
    two_in[128:B] = jnp.where(odd, rin[EDGE:], lin[EDGE:])
    beside = jnp.where(odd, lin[:EDGE], rin[:EDGE])
    for n in (0, 1):
        two_in[B + n * 128 : B + (n + 1) * 128] = level_two(beside, n)
    for i, ref in enumerate((rin, lin)):
        for n in (0, 1):
            rows = (2 * i + n) * B
            one_in[rows : rows + 128] = pooled(ref[n * B : (n + 1) * B], 1, n == 0)
            one_in[rows + 128 : rows + B] = ref[2 * B + n * 128 : 2 * B + (n + 1) * 128]


def one_body(s, near, far, one_in, out, one):
    def coarse(cols):
        return [
            (one_in[2 * i * B : (2 * i + 1) * B, cols], one_in[(2 * i + 1) * B : (2 * i + 2) * B, cols], bias)
            for i, bias in enumerate(sides(s))
        ]

    q_one = jnp.concatenate([pooled(near[at * B : (at + 1) * B, PACK:], 1, True) for at in (0, 1)])
    attend_to(one, 0, lambda cols: q_one[:, cols], coarse, B, 2.0)
    for at in (0, 1):
        rows = slice(at * B, (at + 1) * B)
        level_one = spread(one[at * 128 : (at + 1) * 128], B, 1)
        outs, weights = merged([unpacked(near[rows, :PACK]), unpacked(far[rows]), level_one])
        for h in range(HEADS):
            out[rows, h * DH : (h + 1) * DH] = outs[h]
        out[rows, COLS:] = weights


def pair_body(s, two_in, bin_, mine, theirs):
    bias = jnp.where(s[4] == 1, 0.0, ABSENT).astype(F32)
    kept = [
        jnp.concatenate(
            [two_in[B + n * 128 : B + (n + 1) * 128], bin_[n * 128 : (n + 1) * 128]], axis=0
        )
        for n in (0, 1)
    ]
    spans = [slice(h * DH, (h + 1) * DH) for h in range(HEADS)]
    jobs = [(two_in[:B, cols], [(kept[0][:, cols], kept[1][:, cols], bias)]) for cols in spans]
    values = []
    for cols, (o, value) in zip(spans, attend(jobs, 4.0)):
        mine[:, cols] = o[:128]
        theirs[:, cols] = o[128:]
        values.append(value)
    tile = tile_of(values)
    mine[:, COLS:] = tile[:128]
    theirs[:, COLS:] = tile[128:]


def row_pay_body(s, ain, xpay):
    same = s[1] * HEADS
    for j in range(RING):
        xpay[j * ROWS4 : (j + 1) * ROWS4] = ain[j, ROWS4 : 2 * ROWS4]
        xpay[B + j * ROWS4 : B + (j + 1) * ROWS4] = ain[j, 2 * ROWS4 : 3 * ROWS4]
    for j in range(HEADS):
        for n in (0, 1):
            base = 3 * ROWS4 + n * ROWS3
            to = (2 + n) * B + j * ROWS3
            xpay[to : to + ROWS3] = ain[same + j, base : base + ROWS3]


def row_body(s, ain, xin, back):
    half, head = s[1], s[5]
    bias = jnp.where(s[6] == 1, 0.0, ABSENT).astype(F32)
    mine, other = half * HEADS, (1 - half) * HEADS
    base = 3 * ROWS4
    rows3 = lambda at, low: jnp.concatenate(
        [ain[at + j, low : low + ROWS3] for j in range(HEADS)], axis=0
    )
    q4 = jnp.concatenate([ain[j, :ROWS4] for j in range(RING)], axis=0)
    ((o4, value4),) = attend([(q4, [(xin[:B], xin[B : 2 * B], bias)])], 16.0)
    parts = [
        (rows3(mine, base), rows3(mine, base + ROWS3), None),
        (xin[2 * B : 3 * B], xin[3 * B :], bias),
    ]
    ((o3, value3),) = attend([(rows3(other, base), parts)], 8.0)
    row = lax.broadcasted_iota(jnp.int32, (ROWS4 + ROWS3, 128), 0)
    col = lax.broadcasted_iota(jnp.int32, (ROWS4 + ROWS3, 128), 1)
    term = lax.broadcasted_iota(jnp.int32, (16, 128), 0)
    for j in range(RING):
        rows4 = slice(j * ROWS4, (j + 1) * ROWS4)
        rows3 = slice((j % HEADS) * ROWS3, (j % HEADS + 1) * ROWS3)
        back[j, :ROWS4] = o4[rows4]
        back[j, ROWS4 : ROWS4 + ROWS3] = o3[rows3]
        values = jnp.concatenate([value4[rows4], value3[rows3]], axis=0)
        line = jnp.sum(jnp.where(row == col, values, 0.0), axis=0, keepdims=True)
        high = line.astype(BF16).astype(F32)
        middle = (line - high).astype(BF16).astype(F32)
        low = line - high - middle
        three = jnp.where(
            term == 0, high, jnp.where(term == 1, middle, jnp.where(term == 2, low, 0.0))
        )
        back[j, ROWS4 + ROWS3 :] = three.astype(BF16)


def merge_body(s, fine, two, two_back, row_back, mine, send):
    low = (1 - s[1]) * HEADS
    row = lax.broadcasted_iota(jnp.int32, (ROWS4 + ROWS3, 128), 0)
    lane = lax.broadcasted_iota(jnp.int32, (ROWS4 + ROWS3, 128), 1)

    def joined(first, rows):
        tile = jnp.zeros((ROWS4 + ROWS3, 128), F32)
        for g in range(HEADS):
            three = row_back[first + g, ROWS4 + ROWS3 :].astype(F32)
            line = jnp.sum(three, axis=0, keepdims=True)
            column = jnp.sum(jnp.where(row == lane, line, 0.0), axis=1, keepdims=True)
            tile = jnp.where(lane == g, column, tile)
        o = [row_back[first + g, rows] for g in range(HEADS)]
        return jnp.concatenate(o + [packed_tile(tile[rows])], axis=1)

    four = [joined(side * HEADS, slice(0, ROWS4)) for side in (0, 1)]
    three = joined(low, slice(ROWS4, ROWS4 + ROWS3))
    terms = [
        unpacked(two[...]),
        unpacked(two_back[...]),
        spread(three, 128, 1),
        spread(four[0], 128, 2),
        spread(four[1], 128, 2),
    ]
    outs, weights = merged(terms)
    coarse = jnp.concatenate([o.astype(BF16) for o in outs] + [packed_tile(weights)], axis=1)
    for at, out in enumerate((mine, send)):
        rows = slice(at * B, (at + 1) * B)
        outs, _ = merged(
            [(fine[rows, :COLS], fine[rows, COLS:]), spread(coarse[at * 64 : (at + 1) * 64], B, 2)]
        )
        for h in range(HEADS):
            out[:, h * DH : (h + 1) * DH] = outs[h].astype(BF16)


def join_body(s, mine, theirs, out, sems):
    low = pl.multiple_of(s[0] * COLS, COLS)
    high = pl.multiple_of((1 - s[0]) * COLS, COLS)
    copies = [
        pltpu.make_async_copy(mine, out.at[:, pl.ds(low, COLS)], sems.at[0]),
        pltpu.make_async_copy(theirs, out.at[:, pl.ds(high, COLS)], sems.at[1]),
    ]
    for copy in copies:
        copy.start()
    for copy in copies:
        copy.wait()


def join(s, mine, theirs):
    return pl.pallas_call(
        join_body,
        out_shape=shaped(B, 2 * COLS),
        in_specs=[pl.BlockSpec(memory_space=pltpu.SMEM)]
        + [pl.BlockSpec(memory_space=pltpu.VMEM)] * 2,
        out_specs=pl.BlockSpec(memory_space=pl.ANY),
        scratch_shapes=[pltpu.SemaphoreType.DMA((2,))],
        compiler_params=pltpu.CompilerParams(vmem_limit_bytes=VMEM_LIMIT),
    )(s, mine, theirs)


def pairs_of(target):
    pairs = []
    for chip in range(CHIPS):
        to = target(chip)
        if 0 <= to < CHIPS:
            pairs += [(2 * chip + core, 2 * to + core) for core in (0, 1)]
    return pairs


SWAP = [(i, i ^ 1) for i in range(2 * CHIPS)]
RIGHT = pairs_of(lambda chip: chip + 1)
LEFT = pairs_of(lambda chip: chip - 1)
PAIR = pairs_of(lambda chip: chip ^ 1)
BOUND = pairs_of(lambda chip: chip - 2 if chip % 2 else chip + 2)
ROW = pairs_of(lambda chip: chip - RING if chip % RING < RING // 2 else chip + RING)
LINES = [
    [2 * (row * RING + z) + core for z in range(RING)]
    for row in range(CHIPS // RING)
    for core in (0, 1)
]


def send_to(x, pairs):
    return lax.ppermute(x, "seq", pairs)


def after(x, y):
    return lax.optimization_barrier((x, y))


def line_swap(x):
    return lax.all_to_all(x, "seq", 0, 0, axis_index_groups=LINES)


def local(query_rows, key_rows, value_rows):
    position = lax.axis_index("seq")
    core = position % 2
    chip = position // 2
    z = chip % RING
    row = chip // RING
    half = z // HEADS
    odd = chip % 2
    has_left = chip >= 1
    has_right = chip <= CHIPS - 2
    has_pair = jnp.where(odd == 1, chip <= CHIPS - 3, chip >= 2)
    has_row = jnp.where(half == 1, row >= 1, row <= CHIPS // RING - 2)
    s = jnp.stack(
        [core, half, has_left, has_right, has_pair, z % HEADS, has_row, odd]
    ).astype(jnp.int32)

    own = half_columns(s, (query_rows, key_rows, value_rows))
    q1, k1, v1 = [send_to(x, SWAP) for x in (query_rows, key_rows, value_rows)]
    (apay,) = call(pool_body, (shaped(RING, SEND, DH),), s, (own, q1, k1, v1), wide=(1, 2, 3))
    ain = line_swap(apay)
    s, _ = after(s, apay)
    pay = shaped(EDGE + 128, COLS)
    rpay, lpay = call(
        edge_body,
        (pay, pay),
        s,
        (own, q1, k1, v1),
        wide=(1, 2, 3),
        extra=[pltpu.VMEM(pay.shape, BF16)] * 2 + [pltpu.SemaphoreType.DMA((2,))],
        slow=True,
    )
    rin = send_to(rpay, RIGHT)
    lin = send_to(lpay, LEFT)
    s, _ = after(s, (rpay, lpay))
    (xpay,) = call(row_pay_body, (shaped(4 * B, DH),), s, (ain,))
    xin = send_to(xpay, ROW)
    s, _ = after(s, xpay)
    (bpay,) = call(block_body, (shaped(B, COLS),), s, (own, k1, v1), wide=(1, 2))
    bin_ = send_to(bpay, BOUND)
    s, _ = after(s, bpay)
    (near,) = call(
        near_body,
        (shaped(2 * B, PACK + COLS),),
        s,
        (own, q1, k1, v1),
        wide=(1, 2, 3),
    )
    s, _ = after(s, near)
    (back,) = call(row_body, (shaped(RING, BACK, DH),), s, (ain, xin))
    row_back = line_swap(back)
    s, _ = after(s, back)
    far, two_in, one_in = call(
        far_body,
        (shaped(2 * B, PACK), shaped(2 * B, COLS), shaped(4 * B, COLS)),
        s,
        (near, rin, lin),
    )
    s, _ = after(s, far)
    two, theirs = call(pair_body, (shaped(128, PACK), shaped(128, PACK)), s, (two_in, bin_))
    two_back = send_to(theirs, PAIR)
    s, _ = after(s, theirs)
    (fine,) = call(
        one_body,
        (jax.ShapeDtypeStruct((2 * B, PACK), F32),),
        s,
        (near, far, one_in),
        extra=[pltpu.VMEM((B, PACK), BF16)],
    )
    mine, send = call(
        merge_body, (shaped(B, COLS), shaped(B, COLS)), s, (fine, two, two_back, row_back)
    )
    return join(s, mine, send_to(send, SWAP))


def solution(mesh):
    spec = P("seq", None)
    return jax.shard_map(
        local, mesh=mesh, in_specs=(spec, spec, spec), out_specs=spec, check_vma=False
    )
```

```python
import functools
import math

import jax
import jax.numpy as jnp
from jax import lax
from jax.experimental import pallas as pl
from jax.experimental.pallas import tpu as pltpu
from jax.sharding import PartitionSpec as P

HEADS = 4
DH = 128
COLS = HEADS * DH
B = 256
PACK = COLS + 128
ABSENT = -1e30
SCALE = math.log2(math.e) / math.sqrt(DH)
F32 = jnp.float32
BF16 = jnp.bfloat16

CHIPS = 128
RING = 8
ROWS4, ROWS3 = 32, 64
SEND = 3 * ROWS4 + 2 * ROWS3
BACK = ROWS4 + ROWS3 + 16
VMEM_LIMIT = 10 * 2**20
EDGE = 3 * B


def shaped(*shape):
    return jax.ShapeDtypeStruct(shape, BF16)


def call(body, outs, scalars, arrays, wide=(), extra=(), slow=False):
    def outer(s, *refs):
        start = pl.multiple_of(s[0] * COLS, COLS)
        refs = [
            ref.at[:, pl.ds(start, COLS)] if i in wide else ref for i, ref in enumerate(refs)
        ]
        body(s, *refs)

    return pl.pallas_call(
        outer,
        out_shape=[pltpu.HBM(o.shape, o.dtype) for o in outs] if slow else outs,
        in_specs=[pl.BlockSpec(memory_space=pltpu.SMEM)]
        + [pl.BlockSpec(memory_space=pltpu.VMEM)] * len(arrays),
        out_specs=[pl.BlockSpec(memory_space=pltpu.HBM if slow else pltpu.VMEM)] * len(outs),
        scratch_shapes=list(extra),
        compiler_params=pltpu.CompilerParams(vmem_limit_bytes=VMEM_LIMIT),
        cost_estimate=pl.CostEstimate(flops=0, bytes_accessed=0, transcendentals=0),
    )(scalars, *arrays)


def half_body(s, q, k, v, out, sems):
    start = pl.multiple_of(s[0] * COLS, COLS)
    copies = [
        pltpu.make_async_copy(ref.at[:, pl.ds(start, COLS)], out.at[i], sems.at[i])
        for i, ref in enumerate((q, k, v))
    ]
    for copy in copies:
        copy.start()
    for copy in copies:
        copy.wait()


def half_columns(s, arrays):
    return pl.pallas_call(
        half_body,
        out_shape=shaped(3, B, COLS),
        in_specs=[pl.BlockSpec(memory_space=pltpu.SMEM)]
        + [pl.BlockSpec(memory_space=pltpu.HBM)] * 3,
        out_specs=pl.BlockSpec(memory_space=pltpu.VMEM),
        scratch_shapes=[pltpu.SemaphoreType.DMA((3,))],
        compiler_params=pltpu.CompilerParams(vmem_limit_bytes=VMEM_LIMIT),
        cost_estimate=pl.CostEstimate(flops=0, bytes_accessed=0, transcendentals=0),
    )(s, *(pltpu.with_memory_space_constraint(x, pltpu.HBM) for x in arrays))


def pool_matrix(rows, width, level, scale):
    row = lax.broadcasted_iota(jnp.int32, (rows, width), 0)
    col = lax.broadcasted_iota(jnp.int32, (rows, width), 1)
    return jnp.where((col >> level) == row, scale, 0.0).astype(BF16)


def spread_matrix(rows, width, level):
    row = lax.broadcasted_iota(jnp.int32, (rows, width), 0)
    col = lax.broadcasted_iota(jnp.int32, (rows, width), 1)
    return jnp.where((row >> level) == col, 1.0, 0.0).astype(BF16)


def pooled(x, level, mean):
    rows = x.shape[0]
    scale = 1.0 / 2**level if mean else 1.0
    matrix = pool_matrix(rows >> level, rows, level, scale)
    return jnp.dot(matrix, x, preferred_element_type=F32).astype(BF16)


def attend(jobs, factor):
    results = []
    scores = []
    for q, parts in jobs:
        row = []
        for k, _, bias in parts:
            s = lax.dot_general(q, k, (((1,), (1,)), ((), ())), preferred_element_type=F32) * SCALE
            row.append(s if bias is None else s + bias)
        scores.append(row)
    tops = [
        functools.reduce(jnp.maximum, [jnp.max(s, axis=1, keepdims=True) for s in row])
        for row in scores
    ]
    weights = [[jnp.exp2(s - m) for s in row] for row, m in zip(scores, tops)]
    totals = [
        functools.reduce(jnp.add, [jnp.sum(w, axis=1, keepdims=True) for w in row]) * factor
        for row in weights
    ]
    for (_, parts), row, m, total in zip(jobs, weights, tops, totals):
        out = None
        for w, (_, v, _) in zip(row, parts):
            o = jnp.dot(w.astype(BF16), v, preferred_element_type=F32)
            out = o if out is None else out + o
        results.append(((out / total).astype(BF16), m + jnp.log2(total)))
    return results


def tile_of(values):
    rows = values[0].shape[0]
    lane = lax.broadcasted_iota(jnp.int32, (rows, 128), 1)
    full = jnp.zeros((rows, 128), F32)
    for h, value in enumerate(values):
        full = jnp.where((lane & 3) == h, value, full)
    high = full.astype(BF16)
    rest = full - high.astype(F32)
    middle = rest.astype(BF16)
    low = (rest - middle.astype(F32)).astype(BF16)
    zero = jnp.zeros((rows, 128), BF16)
    part = lane >> 2
    return jnp.where(part == 0, high, jnp.where(part == 1, middle, jnp.where(part == 2, low, zero)))


def merged(terms):
    top = functools.reduce(jnp.maximum, [t for _, t in terms])
    weights = [jnp.exp2(t - top) for _, t in terms]
    total = functools.reduce(jnp.add, weights)
    inverse = 1.0 / total
    weights = [t * inverse for t in weights]
    outs = []
    for h in range(HEADS):
        cols = slice(h * DH, (h + 1) * DH)
        parts = [o[:, cols] * t[:, h : h + 1] for (o, _), t in zip(terms, weights)]
        outs.append(functools.reduce(jnp.add, parts))
    return outs, top + jnp.log2(total)


def unpacked(values):
    values = values.astype(F32)
    t = values[:, COLS:]
    return values[:, :COLS], t + pltpu.roll(t, 128 - 4, 1) + pltpu.roll(t, 128 - 8, 1)


def packed_tile(full):
    lane = lax.broadcasted_iota(jnp.int32, full.shape, 1)
    full = jnp.where(lane < HEADS, full, 0.0)
    high = full.astype(BF16).astype(F32)
    middle = (full - high).astype(BF16).astype(F32)
    low = (full - high - middle).astype(BF16).astype(F32)
    return (high + pltpu.roll(middle, 4, 1) + pltpu.roll(low, 8, 1)).astype(BF16)


def spread(values, rows, level):
    matrix = spread_matrix(rows, rows >> level, level)
    return unpacked(jnp.dot(matrix, values, preferred_element_type=F32))


def attend_to(out_ref, row, q_of, parts_of, rows, factor, group=2):
    values = []
    for first in range(0, HEADS, group):
        spans = [slice(h * DH, (h + 1) * DH) for h in range(first, first + group)]
        for cols, (o, value) in zip(
            spans, attend([(q_of(cols), parts_of(cols)) for cols in spans], factor)
        ):
            out_ref[row : row + rows, cols] = o
            values.append(value)
    out_ref[row : row + rows, COLS:PACK] = tile_of(values)


def edge_body(s, own, q1, k1, v1, rout, lout, rpay, lpay, sems):
    copies = []
    queries = [pooled(x, 2, True) for x in (own[0], q1[...])]
    for i, (pay, out) in enumerate(((rpay, rout), (lpay, lout))):
        first = s[0] == 1 - i
        for n, ref in enumerate((k1, v1)):
            mine, other = own[1 + n], ref[...]
            pay[n * B : (n + 1) * B] = jnp.where(first, mine, other)
            pay[2 * B + n * 128 : 2 * B + (n + 1) * 128] = pooled(
                jnp.where(first, other, mine), 1, n == 0
            )
        for n, x in enumerate(queries):
            pay[EDGE + n * 64 : EDGE + (n + 1) * 64] = x
        copies.append(pltpu.make_async_copy(pay, out, sems.at[i]))
        copies[-1].start()
    for copy in copies:
        copy.wait()


def pool_body(s, own, q1, k1, v1, apay):
    half = s[1]
    matrices = [
        jnp.concatenate(
            [pool_matrix(B >> level, B, level, 1.0 / 2**level if mean else 1.0) for level in (3, 4)],
            axis=0,
        )
        for mean in (True, False)
    ]
    for at in (0, 1):
        whole = (own[0], own[1], own[2]) if at == 0 else (q1[...], k1[...], v1[...])
        both = [jnp.dot(matrices[n == 2], x, preferred_element_type=F32) for n, x in enumerate(whole)]
        three = [x[: B >> 3].astype(BF16) for x in both]
        four = [x[B >> 3 :].astype(BF16) for x in both]
        for j in range(RING):
            cols = slice((j % HEADS) * DH, (j % HEADS + 1) * DH)
            for n in range(3):
                apay[j, n * ROWS4 + at * 16 : n * ROWS4 + (at + 1) * 16] = four[n][:, cols]
            first = jnp.where(half == j // HEADS, three[1][:, cols], three[0][:, cols])
            base = 3 * ROWS4
            apay[j, base + at * 32 : base + (at + 1) * 32] = first
            base += ROWS3
            apay[j, base + at * 32 : base + (at + 1) * 32] = three[2][:, cols]


def near_body(s, own, q1, k1, v1, out):
    k0, v0 = own.at[1], own.at[2]
    for at, q in enumerate((own.at[0], q1)):
        rows = slice(at * B, (at + 1) * B)
        out[rows, PACK:] = q[...]
        attend_to(
            out,
            at * B,
            lambda cols: q[:, cols],
            lambda cols: [(k0[:, cols], v0[:, cols], None), (k1[:, cols], v1[:, cols], None)],
            B,
            1.0,
        )


def level_two(x, n):
    near = pooled(x[n * B : (n + 1) * B], 2, n == 0)
    far = pooled(x[2 * B + n * 128 : 2 * B + (n + 1) * 128], 1, n == 0)
    return jnp.concatenate([near, far], axis=0)


def block_body(s, own, k1, v1, bpay):
    for n, ref in enumerate((k1, v1)):
        bpay[n * 128 : n * 128 + 64] = pooled(own[1 + n], 2, n == 0)
        bpay[n * 128 + 64 : (n + 1) * 128] = pooled(ref[...], 2, n == 0)


def sides(s):
    left = jnp.where(s[2] == 1, 0.0, ABSENT).astype(F32)
    right = jnp.where(s[3] == 1, 0.0, ABSENT).astype(F32)
    return left, right


def far_body(s, near, rin, lin, out, two_in, one_in):
    first = s[0] == 0
    bias_left, bias_right = sides(s)
    for at in (0, 1):
        rows = slice(at * B, (at + 1) * B)
        left = first if at == 0 else jnp.logical_not(first)
        bias = jnp.where(left, bias_left, bias_right)
        attend_to(
            out,
            at * B,
            lambda cols: near[rows, PACK + cols.start : PACK + cols.stop],
            lambda cols: [
                (
                    jnp.where(left, rin[:B, cols], lin[:B, cols]),
                    jnp.where(left, rin[B : 2 * B, cols], lin[B : 2 * B, cols]),
                    bias,
                )
            ],
            B,
            1.0,
        )


    odd = s[7] == 1
    for at in (0, 1):
        two_in[at * 64 : (at + 1) * 64] = pooled(near[at * B : (at + 1) * B, PACK:], 2, True)
    two_in[128:B] = jnp.where(odd, rin[EDGE:], lin[EDGE:])
    beside = jnp.where(odd, lin[:EDGE], rin[:EDGE])
    for n in (0, 1):
        two_in[B + n * 128 : B + (n + 1) * 128] = level_two(beside, n)
    for i, ref in enumerate((rin, lin)):
        for n in (0, 1):
            rows = (2 * i + n) * B
            one_in[rows : rows + 128] = pooled(ref[n * B : (n + 1) * B], 1, n == 0)
            one_in[rows + 128 : rows + B] = ref[2 * B + n * 128 : 2 * B + (n + 1) * 128]


def one_body(s, near, far, one_in, out, one):
    def coarse(cols):
        return [
            (one_in[2 * i * B : (2 * i + 1) * B, cols], one_in[(2 * i + 1) * B : (2 * i + 2) * B, cols], bias)
            for i, bias in enumerate(sides(s))
        ]

    q_one = jnp.concatenate([pooled(near[at * B : (at + 1) * B, PACK:], 1, True) for at in (0, 1)])
    attend_to(one, 0, lambda cols: q_one[:, cols], coarse, B, 2.0)
    for at in (0, 1):
        rows = slice(at * B, (at + 1) * B)
        level_one = spread(one[at * 128 : (at + 1) * 128], B, 1)
        outs, weights = merged([unpacked(near[rows, :PACK]), unpacked(far[rows]), level_one])
        for h in range(HEADS):
            out[rows, h * DH : (h + 1) * DH] = outs[h]
        out[rows, COLS:] = weights


def pair_body(s, two_in, bin_, mine, theirs):
    bias = jnp.where(s[4] == 1, 0.0, ABSENT).astype(F32)
    kept = [
        jnp.concatenate(
            [two_in[B + n * 128 : B + (n + 1) * 128], bin_[n * 128 : (n + 1) * 128]], axis=0
        )
        for n in (0, 1)
    ]
    spans = [slice(h * DH, (h + 1) * DH) for h in range(HEADS)]
    jobs = [(two_in[:B, cols], [(kept[0][:, cols], kept[1][:, cols], bias)]) for cols in spans]
    values = []
    for cols, (o, value) in zip(spans, attend(jobs, 4.0)):
        mine[:, cols] = o[:128]
        theirs[:, cols] = o[128:]
        values.append(value)
    tile = tile_of(values)
    mine[:, COLS:] = tile[:128]
    theirs[:, COLS:] = tile[128:]


def row_pay_body(s, ain, xpay):
    same = s[1] * HEADS
    for j in range(RING):
        xpay[j * ROWS4 : (j + 1) * ROWS4] = ain[j, ROWS4 : 2 * ROWS4]
        xpay[B + j * ROWS4 : B + (j + 1) * ROWS4] = ain[j, 2 * ROWS4 : 3 * ROWS4]
    for j in range(HEADS):
        for n in (0, 1):
            base = 3 * ROWS4 + n * ROWS3
            to = (2 + n) * B + j * ROWS3
            xpay[to : to + ROWS3] = ain[same + j, base : base + ROWS3]


def row_body(s, ain, xin, back):
    half, head = s[1], s[5]
    bias = jnp.where(s[6] == 1, 0.0, ABSENT).astype(F32)
    mine, other = half * HEADS, (1 - half) * HEADS
    base = 3 * ROWS4
    rows3 = lambda at, low: jnp.concatenate(
        [ain[at + j, low : low + ROWS3] for j in range(HEADS)], axis=0
    )
    q4 = jnp.concatenate([ain[j, :ROWS4] for j in range(RING)], axis=0)
    ((o4, value4),) = attend([(q4, [(xin[:B], xin[B : 2 * B], bias)])], 16.0)
    parts = [
        (rows3(mine, base), rows3(mine, base + ROWS3), None),
        (xin[2 * B : 3 * B], xin[3 * B :], bias),
    ]
    ((o3, value3),) = attend([(rows3(other, base), parts)], 8.0)
    row = lax.broadcasted_iota(jnp.int32, (ROWS4 + ROWS3, 128), 0)
    col = lax.broadcasted_iota(jnp.int32, (ROWS4 + ROWS3, 128), 1)
    term = lax.broadcasted_iota(jnp.int32, (16, 128), 0)
    for j in range(RING):
        rows4 = slice(j * ROWS4, (j + 1) * ROWS4)
        rows3 = slice((j % HEADS) * ROWS3, (j % HEADS + 1) * ROWS3)
        back[j, :ROWS4] = o4[rows4]
        back[j, ROWS4 : ROWS4 + ROWS3] = o3[rows3]
        values = jnp.concatenate([value4[rows4], value3[rows3]], axis=0)
        line = jnp.sum(jnp.where(row == col, values, 0.0), axis=0, keepdims=True)
        high = line.astype(BF16).astype(F32)
        middle = (line - high).astype(BF16).astype(F32)
        low = line - high - middle
        three = jnp.where(
            term == 0, high, jnp.where(term == 1, middle, jnp.where(term == 2, low, 0.0))
        )
        back[j, ROWS4 + ROWS3 :] = three.astype(BF16)


def merge_body(s, fine, two, two_back, row_back, send, kept):
    low = (1 - s[1]) * HEADS
    row = lax.broadcasted_iota(jnp.int32, (ROWS4 + ROWS3, 128), 0)
    lane = lax.broadcasted_iota(jnp.int32, (ROWS4 + ROWS3, 128), 1)

    def joined(first, rows):
        tile = jnp.zeros((ROWS4 + ROWS3, 128), F32)
        for g in range(HEADS):
            three = row_back[first + g, ROWS4 + ROWS3 :].astype(F32)
            line = jnp.sum(three, axis=0, keepdims=True)
            column = jnp.sum(jnp.where(row == lane, line, 0.0), axis=1, keepdims=True)
            tile = jnp.where(lane == g, column, tile)
        o = [row_back[first + g, rows] for g in range(HEADS)]
        return jnp.concatenate(o + [packed_tile(tile[rows])], axis=1)

    four = [joined(side * HEADS, slice(0, ROWS4)) for side in (0, 1)]
    three = joined(low, slice(ROWS4, ROWS4 + ROWS3))
    terms = [
        unpacked(two[...]),
        unpacked(two_back[...]),
        spread(three, 128, 1),
        spread(four[0], 128, 2),
        spread(four[1], 128, 2),
    ]
    outs, weights = merged(terms)
    coarse = jnp.concatenate([o.astype(BF16) for o in outs] + [packed_tile(weights)], axis=1)
    kept[...] = coarse[:64]
    finish(fine, B, coarse[64:], send)


def finish(fine, start, coarse, out):
    rows = slice(start, start + B)
    outs, _ = merged([(fine[rows, :COLS], fine[rows, COLS:]), spread(coarse, B, 2)])
    for h in range(HEADS):
        out[:, h * DH : (h + 1) * DH] = outs[h].astype(BF16)


def own_body(s, fine, kept, out, mine, sem):
    finish(fine, 0, kept[...], mine)
    low = pl.multiple_of(s[0] * COLS, COLS)
    copy = pltpu.make_async_copy(mine, out.at[:, pl.ds(low, COLS)], sem)
    copy.start()
    copy.wait()


def own_columns(s, fine, kept):
    return pl.pallas_call(
        own_body,
        out_shape=shaped(B, 2 * COLS),
        in_specs=[pl.BlockSpec(memory_space=pltpu.SMEM)]
        + [pl.BlockSpec(memory_space=pltpu.VMEM)] * 2,
        out_specs=pl.BlockSpec(memory_space=pl.ANY),
        scratch_shapes=[pltpu.VMEM((B, COLS), BF16), pltpu.SemaphoreType.DMA],
        compiler_params=pltpu.CompilerParams(vmem_limit_bytes=VMEM_LIMIT),
        cost_estimate=pl.CostEstimate(flops=0, bytes_accessed=0, transcendentals=0),
    )(s, fine, kept)


def join_body(s, part, theirs, out, sem):
    high = pl.multiple_of((1 - s[0]) * COLS, COLS)
    copy = pltpu.make_async_copy(theirs, out.at[:, pl.ds(high, COLS)], sem)
    copy.start()
    copy.wait()


def join(s, part, theirs):
    return pl.pallas_call(
        join_body,
        out_shape=shaped(B, 2 * COLS),
        in_specs=[
            pl.BlockSpec(memory_space=pltpu.SMEM),
            pl.BlockSpec(memory_space=pl.ANY),
            pl.BlockSpec(memory_space=pltpu.VMEM),
        ],
        out_specs=pl.BlockSpec(memory_space=pl.ANY),
        scratch_shapes=[pltpu.SemaphoreType.DMA],
        input_output_aliases={1: 0},
        compiler_params=pltpu.CompilerParams(vmem_limit_bytes=VMEM_LIMIT),
        cost_estimate=pl.CostEstimate(flops=0, bytes_accessed=0, transcendentals=0),
    )(s, part, theirs)


def pairs_of(target):
    pairs = []
    for chip in range(CHIPS):
        to = target(chip)
        if 0 <= to < CHIPS:
            pairs += [(2 * chip + core, 2 * to + core) for core in (0, 1)]
    return pairs


SWAP = [(i, i ^ 1) for i in range(2 * CHIPS)]
RIGHT = pairs_of(lambda chip: chip + 1)
LEFT = pairs_of(lambda chip: chip - 1)
PAIR = pairs_of(lambda chip: chip ^ 1)
BOUND = pairs_of(lambda chip: chip - 2 if chip % 2 else chip + 2)
ROW = pairs_of(lambda chip: chip - RING if chip % RING < RING // 2 else chip + RING)
LINES = [
    [2 * (row * RING + z) + core for z in range(RING)]
    for row in range(CHIPS // RING)
    for core in (0, 1)
]


def send_to(x, pairs):
    return lax.ppermute(x, "seq", pairs)


def after(x, y):
    return lax.optimization_barrier((x, y))


def line_swap(x):
    return lax.all_to_all(x, "seq", 0, 0, axis_index_groups=LINES)


def local(query_rows, key_rows, value_rows):
    position = lax.axis_index("seq")
    core = position % 2
    chip = position // 2
    z = chip % RING
    row = chip // RING
    half = z // HEADS
    odd = chip % 2
    has_left = chip >= 1
    has_right = chip <= CHIPS - 2
    has_pair = jnp.where(odd == 1, chip <= CHIPS - 3, chip >= 2)
    has_row = jnp.where(half == 1, row >= 1, row <= CHIPS // RING - 2)
    s = jnp.stack(
        [core, half, has_left, has_right, has_pair, z % HEADS, has_row, odd]
    ).astype(jnp.int32)

    own = half_columns(s, (query_rows, key_rows, value_rows))
    q1, k1, v1 = [send_to(x, SWAP) for x in (query_rows, key_rows, value_rows)]
    (apay,) = call(pool_body, (shaped(RING, SEND, DH),), s, (own, q1, k1, v1), wide=(1, 2, 3))
    ain = line_swap(apay)
    s, _ = after(s, apay)
    pay = shaped(EDGE + 128, COLS)
    rpay, lpay = call(
        edge_body,
        (pay, pay),
        s,
        (own, q1, k1, v1),
        wide=(1, 2, 3),
        extra=[pltpu.VMEM(pay.shape, BF16)] * 2 + [pltpu.SemaphoreType.DMA((2,))],
        slow=True,
    )
    rin = send_to(rpay, RIGHT)
    lin = send_to(lpay, LEFT)
    s, _ = after(s, (rpay, lpay))
    (near,) = call(
        near_body,
        (shaped(2 * B, PACK + COLS),),
        s,
        (own, q1, k1, v1),
        wide=(1, 2, 3),
    )
    s, _ = after(s, near)
    (xpay,) = call(row_pay_body, (shaped(4 * B, DH),), s, (ain,))
    xin = send_to(xpay, ROW)
    s, _ = after(s, xpay)
    (bpay,) = call(block_body, (shaped(B, COLS),), s, (own, k1, v1), wide=(1, 2))
    bin_ = send_to(bpay, BOUND)
    s, _ = after(s, bpay)
    (back,) = call(row_body, (shaped(RING, BACK, DH),), s, (ain, xin))
    row_back = line_swap(back)
    s, _ = after(s, back)
    far, two_in, one_in = call(
        far_body,
        (shaped(2 * B, PACK), shaped(2 * B, COLS), shaped(4 * B, COLS)),
        s,
        (near, rin, lin),
    )
    s, _ = after(s, far)
    two, theirs = call(pair_body, (shaped(128, PACK), shaped(128, PACK)), s, (two_in, bin_))
    two_back = send_to(theirs, PAIR)
    s, _ = after(s, theirs)
    (fine,) = call(
        one_body,
        (jax.ShapeDtypeStruct((2 * B, PACK), F32),),
        s,
        (near, far, one_in),
        extra=[pltpu.VMEM((B, PACK), BF16)],
    )
    send, kept = call(
        merge_body, (shaped(B, COLS), shaped(64, PACK)), s, (fine, two, two_back, row_back)
    )
    theirs = send_to(send, SWAP)
    s, _ = after(s, send)
    return join(s, own_columns(s, fine, kept), theirs)


def solution(mesh):
    spec = P("seq", None)
    return jax.shard_map(
        local, mesh=mesh, in_specs=(spec, spec, spec), out_specs=spec, check_vma=False
    )
```

```python
import functools
import math

import jax
import jax.numpy as jnp
from jax import lax
from jax.experimental import pallas as pl
from jax.experimental.pallas import tpu as pltpu
from jax.sharding import PartitionSpec as P

HEADS = 4
DH = 128
COLS = HEADS * DH
B = 256
PACK = COLS + 128
ABSENT = -1e30
SCALE = math.log2(math.e) / math.sqrt(DH)
F32 = jnp.float32
BF16 = jnp.bfloat16

CHIPS = 128
RING = 8
ROWS4, ROWS3 = 32, 64
SEND = 3 * ROWS4 + 2 * ROWS3
BACK = ROWS4 + ROWS3 + 16
VMEM_LIMIT = 10 * 2**20
EDGE = 3 * B


def shaped(*shape):
    return jax.ShapeDtypeStruct(shape, BF16)


def call(body, outs, scalars, arrays, wide=(), extra=(), slow=False):
    def outer(s, *refs):
        start = pl.multiple_of(s[0] * COLS, COLS)
        refs = [
            ref.at[:, pl.ds(start, COLS)] if i in wide else ref for i, ref in enumerate(refs)
        ]
        body(s, *refs)

    return pl.pallas_call(
        outer,
        out_shape=[pltpu.HBM(o.shape, o.dtype) for o in outs] if slow else outs,
        in_specs=[pl.BlockSpec(memory_space=pltpu.SMEM)]
        + [pl.BlockSpec(memory_space=pltpu.VMEM)] * len(arrays),
        out_specs=[pl.BlockSpec(memory_space=pltpu.HBM if slow else pltpu.VMEM)] * len(outs),
        scratch_shapes=list(extra),
        compiler_params=pltpu.CompilerParams(vmem_limit_bytes=VMEM_LIMIT),
        cost_estimate=pl.CostEstimate(flops=0, bytes_accessed=0, transcendentals=0),
    )(scalars, *arrays)


def half_body(s, q, k, v, out, sems):
    start = pl.multiple_of(s[0] * COLS, COLS)
    copies = [
        pltpu.make_async_copy(ref.at[:, pl.ds(start, COLS)], out.at[i], sems.at[i])
        for i, ref in enumerate((q, k, v))
    ]
    for copy in copies:
        copy.start()
    for copy in copies:
        copy.wait()


def half_columns(s, arrays):
    return pl.pallas_call(
        half_body,
        out_shape=shaped(3, B, COLS),
        in_specs=[pl.BlockSpec(memory_space=pltpu.SMEM)]
        + [pl.BlockSpec(memory_space=pltpu.HBM)] * 3,
        out_specs=pl.BlockSpec(memory_space=pltpu.VMEM),
        scratch_shapes=[pltpu.SemaphoreType.DMA((3,))],
        compiler_params=pltpu.CompilerParams(vmem_limit_bytes=VMEM_LIMIT),
        cost_estimate=pl.CostEstimate(flops=0, bytes_accessed=0, transcendentals=0),
    )(s, *(pltpu.with_memory_space_constraint(x, pltpu.HBM) for x in arrays))


def pool_matrix(rows, width, level, scale):
    row = lax.broadcasted_iota(jnp.int32, (rows, width), 0)
    col = lax.broadcasted_iota(jnp.int32, (rows, width), 1)
    return jnp.where((col >> level) == row, scale, 0.0).astype(BF16)


def spread_matrix(rows, width, level):
    row = lax.broadcasted_iota(jnp.int32, (rows, width), 0)
    col = lax.broadcasted_iota(jnp.int32, (rows, width), 1)
    return jnp.where((row >> level) == col, 1.0, 0.0).astype(BF16)


def pooled(x, level, mean):
    rows = x.shape[0]
    scale = 1.0 / 2**level if mean else 1.0
    matrix = pool_matrix(rows >> level, rows, level, scale)
    return jnp.dot(matrix, x, preferred_element_type=F32).astype(BF16)


def attend(jobs, factor):
    results = []
    scores = []
    for q, parts in jobs:
        row = []
        for k, _, bias in parts:
            s = lax.dot_general(q, k, (((1,), (1,)), ((), ())), preferred_element_type=F32) * SCALE
            row.append(s if bias is None else s + bias)
        scores.append(row)
    tops = [
        functools.reduce(jnp.maximum, [jnp.max(s, axis=1, keepdims=True) for s in row])
        for row in scores
    ]
    weights = [[jnp.exp2(s - m) for s in row] for row, m in zip(scores, tops)]
    totals = [
        functools.reduce(jnp.add, [jnp.sum(w, axis=1, keepdims=True) for w in row]) * f
        for row, f in zip(weights, factor if isinstance(factor, tuple) else (factor,) * len(jobs))
    ]
    for (_, parts), row, m, total in zip(jobs, weights, tops, totals):
        out = None
        for w, (_, v, _) in zip(row, parts):
            o = jnp.dot(w.astype(BF16), v, preferred_element_type=F32)
            out = o if out is None else out + o
        results.append(((out / total).astype(BF16), m + jnp.log2(total)))
    return results


def tile_of(values):
    rows = values[0].shape[0]
    lane = lax.broadcasted_iota(jnp.int32, (rows, 128), 1)
    full = jnp.zeros((rows, 128), F32)
    for h, value in enumerate(values):
        full = jnp.where((lane & 3) == h, value, full)
    high = full.astype(BF16)
    rest = full - high.astype(F32)
    middle = rest.astype(BF16)
    low = (rest - middle.astype(F32)).astype(BF16)
    zero = jnp.zeros((rows, 128), BF16)
    part = lane >> 2
    return jnp.where(part == 0, high, jnp.where(part == 1, middle, jnp.where(part == 2, low, zero)))


def merged(terms):
    top = functools.reduce(jnp.maximum, [t for _, t in terms])
    weights = [jnp.exp2(t - top) for _, t in terms]
    total = functools.reduce(jnp.add, weights)
    inverse = 1.0 / total
    weights = [t * inverse for t in weights]
    outs = []
    for h in range(HEADS):
        cols = slice(h * DH, (h + 1) * DH)
        parts = [o[:, cols] * t[:, h : h + 1] for (o, _), t in zip(terms, weights)]
        outs.append(functools.reduce(jnp.add, parts))
    return outs, top + jnp.log2(total)


def unpacked(values):
    values = values.astype(F32)
    t = values[:, COLS:]
    return values[:, :COLS], t + pltpu.roll(t, 128 - 4, 1) + pltpu.roll(t, 128 - 8, 1)


def packed_tile(full):
    lane = lax.broadcasted_iota(jnp.int32, full.shape, 1)
    full = jnp.where(lane < HEADS, full, 0.0)
    high = full.astype(BF16).astype(F32)
    middle = (full - high).astype(BF16).astype(F32)
    low = (full - high - middle).astype(BF16).astype(F32)
    return (high + pltpu.roll(middle, 4, 1) + pltpu.roll(low, 8, 1)).astype(BF16)


def spread(values, rows, level):
    matrix = spread_matrix(rows, rows >> level, level)
    return unpacked(jnp.dot(matrix, values, preferred_element_type=F32))


def attend_to(out_ref, row, q_of, parts_of, rows, factor, group=2):
    values = []
    for first in range(0, HEADS, group):
        spans = [slice(h * DH, (h + 1) * DH) for h in range(first, first + group)]
        for cols, (o, value) in zip(
            spans, attend([(q_of(cols), parts_of(cols)) for cols in spans], factor)
        ):
            out_ref[row : row + rows, cols] = o
            values.append(value)
    out_ref[row : row + rows, COLS:PACK] = tile_of(values)


def edge_body(s, own, q1, k1, v1, rout, lout, rpay, lpay, sems):
    copies = []
    queries = [pooled(x, 2, True) for x in (own[0], q1[...])]
    for i, (pay, out) in enumerate(((rpay, rout), (lpay, lout))):
        first = s[0] == 1 - i
        for n, ref in enumerate((k1, v1)):
            mine, other = own[1 + n], ref[...]
            pay[n * B : (n + 1) * B] = jnp.where(first, mine, other)
            pay[2 * B + n * 128 : 2 * B + (n + 1) * 128] = pooled(
                jnp.where(first, other, mine), 1, n == 0
            )
        for n, x in enumerate(queries):
            pay[EDGE + n * 64 : EDGE + (n + 1) * 64] = x
        copies.append(pltpu.make_async_copy(pay, out, sems.at[i]))
        copies[-1].start()
    for copy in copies:
        copy.wait()


def pool_body(s, own, q1, k1, v1, apay):
    half = s[1]
    matrices = [
        jnp.concatenate(
            [pool_matrix(B >> level, B, level, 1.0 / 2**level if mean else 1.0) for level in (3, 4)],
            axis=0,
        )
        for mean in (True, False)
    ]
    for at in (0, 1):
        whole = (own[0], own[1], own[2]) if at == 0 else (q1[...], k1[...], v1[...])
        both = [jnp.dot(matrices[n == 2], x, preferred_element_type=F32) for n, x in enumerate(whole)]
        three = [x[: B >> 3].astype(BF16) for x in both]
        four = [x[B >> 3 :].astype(BF16) for x in both]
        for j in range(RING):
            cols = slice((j % HEADS) * DH, (j % HEADS + 1) * DH)
            for n in range(3):
                apay[j, n * ROWS4 + at * 16 : n * ROWS4 + (at + 1) * 16] = four[n][:, cols]
            first = jnp.where(half == j // HEADS, three[1][:, cols], three[0][:, cols])
            base = 3 * ROWS4
            apay[j, base + at * 32 : base + (at + 1) * 32] = first
            base += ROWS3
            apay[j, base + at * 32 : base + (at + 1) * 32] = three[2][:, cols]


def near_body(s, own, q1, k1, v1, out):
    k0, v0 = own.at[1], own.at[2]
    for at, q in enumerate((own.at[0], q1)):
        rows = slice(at * B, (at + 1) * B)
        out[rows, PACK:] = q[...]
        attend_to(
            out,
            at * B,
            lambda cols: q[:, cols],
            lambda cols: [(k0[:, cols], v0[:, cols], None), (k1[:, cols], v1[:, cols], None)],
            B,
            1.0,
        )


def level_two(x, n):
    near = pooled(x[n * B : (n + 1) * B], 2, n == 0)
    far = pooled(x[2 * B + n * 128 : 2 * B + (n + 1) * 128], 1, n == 0)
    return jnp.concatenate([near, far], axis=0)


def block_body(s, own, k1, v1, bpay):
    for n, ref in enumerate((k1, v1)):
        bpay[n * 128 : n * 128 + 64] = pooled(own[1 + n], 2, n == 0)
        bpay[n * 128 + 64 : (n + 1) * 128] = pooled(ref[...], 2, n == 0)


def sides(s):
    left = jnp.where(s[2] == 1, 0.0, ABSENT).astype(F32)
    right = jnp.where(s[3] == 1, 0.0, ABSENT).astype(F32)
    return left, right


def far_body(s, near, rin, lin, out, two_in, one_in):
    first = s[0] == 0
    bias_left, bias_right = sides(s)
    for at in (0, 1):
        rows = slice(at * B, (at + 1) * B)
        left = first if at == 0 else jnp.logical_not(first)
        bias = jnp.where(left, bias_left, bias_right)
        attend_to(
            out,
            at * B,
            lambda cols: near[rows, PACK + cols.start : PACK + cols.stop],
            lambda cols: [
                (
                    jnp.where(left, rin[:B, cols], lin[:B, cols]),
                    jnp.where(left, rin[B : 2 * B, cols], lin[B : 2 * B, cols]),
                    bias,
                )
            ],
            B,
            1.0,
        )


    odd = s[7] == 1
    for at in (0, 1):
        two_in[at * 64 : (at + 1) * 64] = pooled(near[at * B : (at + 1) * B, PACK:], 2, True)
    two_in[128:B] = jnp.where(odd, rin[EDGE:], lin[EDGE:])
    beside = jnp.where(odd, lin[:EDGE], rin[:EDGE])
    for n in (0, 1):
        two_in[B + n * 128 : B + (n + 1) * 128] = level_two(beside, n)
    for i, ref in enumerate((rin, lin)):
        for n in (0, 1):
            rows = (2 * i + n) * B
            one_in[rows : rows + 128] = pooled(ref[n * B : (n + 1) * B], 1, n == 0)
            one_in[rows + 128 : rows + B] = ref[2 * B + n * 128 : 2 * B + (n + 1) * 128]


def one_body(s, near, far, one_in, out, one):
    def coarse(cols):
        return [
            (one_in[2 * i * B : (2 * i + 1) * B, cols], one_in[(2 * i + 1) * B : (2 * i + 2) * B, cols], bias)
            for i, bias in enumerate(sides(s))
        ]

    q_one = jnp.concatenate([pooled(near[at * B : (at + 1) * B, PACK:], 1, True) for at in (0, 1)])
    attend_to(one, 0, lambda cols: q_one[:, cols], coarse, B, 2.0)
    for at in (0, 1):
        rows = slice(at * B, (at + 1) * B)
        level_one = spread(one[at * 128 : (at + 1) * 128], B, 1)
        outs, weights = merged([unpacked(near[rows, :PACK]), unpacked(far[rows]), level_one])
        for h in range(HEADS):
            out[rows, h * DH : (h + 1) * DH] = outs[h]
        out[rows, COLS:] = weights


def pair_body(s, two_in, bin_, mine, theirs):
    bias = jnp.where(s[4] == 1, 0.0, ABSENT).astype(F32)
    kept = [
        jnp.concatenate(
            [two_in[B + n * 128 : B + (n + 1) * 128], bin_[n * 128 : (n + 1) * 128]], axis=0
        )
        for n in (0, 1)
    ]
    spans = [slice(h * DH, (h + 1) * DH) for h in range(HEADS)]
    jobs = [(two_in[:B, cols], [(kept[0][:, cols], kept[1][:, cols], bias)]) for cols in spans]
    values = []
    for cols, (o, value) in zip(spans, attend(jobs, 4.0)):
        mine[:, cols] = o[:128]
        theirs[:, cols] = o[128:]
        values.append(value)
    tile = tile_of(values)
    mine[:, COLS:] = tile[:128]
    theirs[:, COLS:] = tile[128:]


def row_pay_body(s, ain, xpay):
    same = s[1] * HEADS
    for j in range(RING):
        xpay[j * ROWS4 : (j + 1) * ROWS4] = ain[j, ROWS4 : 2 * ROWS4]
        xpay[B + j * ROWS4 : B + (j + 1) * ROWS4] = ain[j, 2 * ROWS4 : 3 * ROWS4]
    for j in range(HEADS):
        for n in (0, 1):
            base = 3 * ROWS4 + n * ROWS3
            to = (2 + n) * B + j * ROWS3
            xpay[to : to + ROWS3] = ain[same + j, base : base + ROWS3]


def row_body(s, ain, xin, back):
    half, head = s[1], s[5]
    bias = jnp.where(s[6] == 1, 0.0, ABSENT).astype(F32)
    mine, other = half * HEADS, (1 - half) * HEADS
    base = 3 * ROWS4
    rows3 = lambda at, low: jnp.concatenate(
        [ain[at + j, low : low + ROWS3] for j in range(HEADS)], axis=0
    )
    q4 = jnp.concatenate([ain[j, :ROWS4] for j in range(RING)], axis=0)
    job4 = (q4, [(xin[:B], xin[B : 2 * B], bias)])
    parts = [
        (rows3(mine, base), rows3(mine, base + ROWS3), None),
        (xin[2 * B : 3 * B], xin[3 * B :], bias),
    ]
    (o4, value4), (o3, value3) = attend([job4, (rows3(other, base), parts)], (16.0, 8.0))
    row = lax.broadcasted_iota(jnp.int32, (ROWS4 + ROWS3, 128), 0)
    col = lax.broadcasted_iota(jnp.int32, (ROWS4 + ROWS3, 128), 1)
    term = lax.broadcasted_iota(jnp.int32, (16, 128), 0)
    for j in range(RING):
        rows4 = slice(j * ROWS4, (j + 1) * ROWS4)
        rows3 = slice((j % HEADS) * ROWS3, (j % HEADS + 1) * ROWS3)
        back[j, :ROWS4] = o4[rows4]
        back[j, ROWS4 : ROWS4 + ROWS3] = o3[rows3]
        values = jnp.concatenate([value4[rows4], value3[rows3]], axis=0)
        line = jnp.sum(jnp.where(row == col, values, 0.0), axis=0, keepdims=True)
        high = line.astype(BF16).astype(F32)
        middle = (line - high).astype(BF16).astype(F32)
        low = line - high - middle
        three = jnp.where(
            term == 0, high, jnp.where(term == 1, middle, jnp.where(term == 2, low, 0.0))
        )
        back[j, ROWS4 + ROWS3 :] = three.astype(BF16)


def merge_body(s, fine, two, two_back, row_back, send, kept):
    low = (1 - s[1]) * HEADS
    row = lax.broadcasted_iota(jnp.int32, (ROWS4 + ROWS3, 128), 0)
    lane = lax.broadcasted_iota(jnp.int32, (ROWS4 + ROWS3, 128), 1)

    def joined(first, rows):
        tile = jnp.zeros((ROWS4 + ROWS3, 128), F32)
        for g in range(HEADS):
            three = row_back[first + g, ROWS4 + ROWS3 :].astype(F32)
            line = jnp.sum(three, axis=0, keepdims=True)
            column = jnp.sum(jnp.where(row == lane, line, 0.0), axis=1, keepdims=True)
            tile = jnp.where(lane == g, column, tile)
        o = [row_back[first + g, rows] for g in range(HEADS)]
        return jnp.concatenate(o + [packed_tile(tile[rows])], axis=1)

    four = [joined(side * HEADS, slice(0, ROWS4)) for side in (0, 1)]
    three = joined(low, slice(ROWS4, ROWS4 + ROWS3))
    terms = [
        unpacked(two[...]),
        unpacked(two_back[...]),
        spread(three, 128, 1),
        spread(four[0], 128, 2),
        spread(four[1], 128, 2),
    ]
    outs, weights = merged(terms)
    coarse = jnp.concatenate([o.astype(BF16) for o in outs] + [packed_tile(weights)], axis=1)
    kept[...] = coarse[:64]
    finish(fine, B, coarse[64:], send)


def finish(fine, start, coarse, out):
    rows = slice(start, start + B)
    outs, _ = merged([(fine[rows, :COLS], fine[rows, COLS:]), spread(coarse, B, 2)])
    for h in range(HEADS):
        out[:, h * DH : (h + 1) * DH] = outs[h].astype(BF16)


def own_body(s, fine, kept, out, mine, sem):
    finish(fine, 0, kept[...], mine)
    low = pl.multiple_of(s[0] * COLS, COLS)
    copy = pltpu.make_async_copy(mine, out.at[:, pl.ds(low, COLS)], sem)
    copy.start()
    copy.wait()


def own_columns(s, fine, kept):
    return pl.pallas_call(
        own_body,
        out_shape=shaped(B, 2 * COLS),
        in_specs=[pl.BlockSpec(memory_space=pltpu.SMEM)]
        + [pl.BlockSpec(memory_space=pltpu.VMEM)] * 2,
        out_specs=pl.BlockSpec(memory_space=pl.ANY),
        scratch_shapes=[pltpu.VMEM((B, COLS), BF16), pltpu.SemaphoreType.DMA],
        compiler_params=pltpu.CompilerParams(vmem_limit_bytes=VMEM_LIMIT),
        cost_estimate=pl.CostEstimate(flops=0, bytes_accessed=0, transcendentals=0),
    )(s, fine, kept)


def join_body(s, part, theirs, out, sem):
    high = pl.multiple_of((1 - s[0]) * COLS, COLS)
    copy = pltpu.make_async_copy(theirs, out.at[:, pl.ds(high, COLS)], sem)
    copy.start()
    copy.wait()


def join(s, part, theirs):
    return pl.pallas_call(
        join_body,
        out_shape=shaped(B, 2 * COLS),
        in_specs=[
            pl.BlockSpec(memory_space=pltpu.SMEM),
            pl.BlockSpec(memory_space=pl.ANY),
            pl.BlockSpec(memory_space=pltpu.VMEM),
        ],
        out_specs=pl.BlockSpec(memory_space=pl.ANY),
        scratch_shapes=[pltpu.SemaphoreType.DMA],
        input_output_aliases={1: 0},
        compiler_params=pltpu.CompilerParams(vmem_limit_bytes=VMEM_LIMIT),
        cost_estimate=pl.CostEstimate(flops=0, bytes_accessed=0, transcendentals=0),
    )(s, part, theirs)


def pairs_of(target):
    pairs = []
    for chip in range(CHIPS):
        to = target(chip)
        if 0 <= to < CHIPS:
            pairs += [(2 * chip + core, 2 * to + core) for core in (0, 1)]
    return pairs


SWAP = [(i, i ^ 1) for i in range(2 * CHIPS)]
RIGHT = pairs_of(lambda chip: chip + 1)
LEFT = pairs_of(lambda chip: chip - 1)
PAIR = pairs_of(lambda chip: chip ^ 1)
BOUND = pairs_of(lambda chip: chip - 2 if chip % 2 else chip + 2)
ROW = pairs_of(lambda chip: chip - RING if chip % RING < RING // 2 else chip + RING)
LINES = [
    [2 * (row * RING + z) + core for z in range(RING)]
    for row in range(CHIPS // RING)
    for core in (0, 1)
]


def send_to(x, pairs):
    return lax.ppermute(x, "seq", pairs)


def after(x, y):
    return lax.optimization_barrier((x, y))


def line_swap(x):
    return lax.all_to_all(x, "seq", 0, 0, axis_index_groups=LINES)


def local(query_rows, key_rows, value_rows):
    position = lax.axis_index("seq")
    core = position % 2
    chip = position // 2
    z = chip % RING
    row = chip // RING
    half = z // HEADS
    odd = chip % 2
    has_left = chip >= 1
    has_right = chip <= CHIPS - 2
    has_pair = jnp.where(odd == 1, chip <= CHIPS - 3, chip >= 2)
    has_row = jnp.where(half == 1, row >= 1, row <= CHIPS // RING - 2)
    s = jnp.stack(
        [core, half, has_left, has_right, has_pair, z % HEADS, has_row, odd]
    ).astype(jnp.int32)

    own = half_columns(s, (query_rows, key_rows, value_rows))
    q1, k1, v1 = [send_to(x, SWAP) for x in (query_rows, key_rows, value_rows)]
    (apay,) = call(pool_body, (shaped(RING, SEND, DH),), s, (own, q1, k1, v1), wide=(1, 2, 3))
    ain = line_swap(apay)
    s, _ = after(s, apay)
    pay = shaped(EDGE + 128, COLS)
    rpay, lpay = call(
        edge_body,
        (pay, pay),
        s,
        (own, q1, k1, v1),
        wide=(1, 2, 3),
        extra=[pltpu.VMEM(pay.shape, BF16)] * 2 + [pltpu.SemaphoreType.DMA((2,))],
        slow=True,
    )
    rin = send_to(rpay, RIGHT)
    lin = send_to(lpay, LEFT)
    s, _ = after(s, (rpay, lpay))
    (near,) = call(
        near_body,
        (shaped(2 * B, PACK + COLS),),
        s,
        (own, q1, k1, v1),
        wide=(1, 2, 3),
    )
    s, _ = after(s, near)
    (xpay,) = call(row_pay_body, (shaped(4 * B, DH),), s, (ain,))
    xin = send_to(xpay, ROW)
    s, _ = after(s, xpay)
    (bpay,) = call(block_body, (shaped(B, COLS),), s, (own, k1, v1), wide=(1, 2))
    bin_ = send_to(bpay, BOUND)
    s, _ = after(s, bpay)
    (back,) = call(row_body, (shaped(RING, BACK, DH),), s, (ain, xin))
    row_back = line_swap(back)
    s, _ = after(s, back)
    far, two_in, one_in = call(
        far_body,
        (shaped(2 * B, PACK), shaped(2 * B, COLS), shaped(4 * B, COLS)),
        s,
        (near, rin, lin),
    )
    s, _ = after(s, far)
    two, theirs = call(pair_body, (shaped(128, PACK), shaped(128, PACK)), s, (two_in, bin_))
    two_back = send_to(theirs, PAIR)
    s, _ = after(s, theirs)
    (fine,) = call(
        one_body,
        (jax.ShapeDtypeStruct((2 * B, PACK), F32),),
        s,
        (near, far, one_in),
        extra=[pltpu.VMEM((B, PACK), BF16)],
    )
    send, kept = call(
        merge_body, (shaped(B, COLS), shaped(64, PACK)), s, (fine, two, two_back, row_back)
    )
    theirs = send_to(send, SWAP)
    s, _ = after(s, send)
    return join(s, own_columns(s, fine, kept), theirs)


def solution(mesh):
    spec = P("seq", None)
    return jax.shard_map(
        local, mesh=mesh, in_specs=(spec, spec, spec), out_specs=spec, check_vma=False
    )
```
